512 devices in a mesh: dp: 8 (over z_hi, y), seq: 64 (over x, z_lo, core).
Axes of the slice: x: 4, y: 4, z: 16 (z_hi: 2, z_lo: 8; z = z_hi * 8 + z_lo), core: 2. Of those that a mesh axis runs over, the one named last changes fastest.
Arguments:
- features: bfloat16 [65536, 320], P(('dp', 'seq')), parts along dimension 0, may hold values from -40 to 40
- hint: bfloat16 [65536, 320], P(('dp', 'seq')), parts along dimension 0, may hold values from -6 to 6
- conv_weight: bfloat16 [3, 3, 320, 320], replicated, may hold values from -0.109375 to 0.109375
- conv_bias: float32 [320], replicated, may hold values from -3 to 3
- zero_weight: bfloat16 [320, 320], replicated, may hold values from -0.3125 to 0.3125
- zero_bias: float32 [320], replicated, may hold values from -2 to 2
- group_gain: float32 [320], replicated, may hold values from 0.5 to 1.5
- proj_in: bfloat16 [320, 320], replicated, may hold values from -0.3125 to 0.3125
- norm_gain: float32 [320], replicated, may hold values from 0.5 to 1.5
- query_weight: bfloat16 [320, 320], replicated, may hold values from -2 to 2
- key_weight: bfloat16 [320, 320], replicated, may hold values from -2 to 2
- value_weight: bfloat16 [320, 320], replicated, may hold values from -0.3125 to 0.3125
- attn_out: bfloat16 [320, 320], replicated, may hold values from -0.3125 to 0.3125
- proj_out: bfloat16 [320, 320], replicated, may hold values from -0.3125 to 0.3125
Outputs:
- block_out: bfloat16 [65536, 320], P(('dp', 'seq')), parts along dimension 0
The draws below stay inside these ranges and needn't reach their ends.
There are 8 independent parts, one for each index of `dp`. The reference program is written for one: setup_inputs(seed, part) draws one part's arguments, and reference() takes and returns one part's arrays. A program takes and returns all parts, laid end to end along the dimension named above; an argument that names none is the same for every part. Nothing has to cross between parts.
All inputs are finite; a program needn't handle non-finite values.
Results may differ from the reference program's by a relative error of at most 0.023.
Values may be sent and summed in bfloat16 or wider, within the bound.
No kernel may reach another device: no remote copies, remote signals or barrier semaphores. Data moves between devices by JAX's collectives and lax.ppermute only.
A program may use at most 64 MiB of HBM per device.

```python
import math
import jax
import jax.numpy as jnp
from jax import lax

C = 320
HEADS = 8
GROUPS = 32
WIDTH = 128
SEQ = 8192


def draw_features(key, part):
    sub_keys = [jax.random.fold_in(key, 11 + index) for index in range(8)]
    position = jnp.arange(SEQ, dtype=jnp.float32) / (SEQ - 1)
    noise_vals = jnp.clip(jax.random.normal(sub_keys[0], (SEQ, C), jnp.float32), -4.0, 4.0)
    rise_row = 1.0 + 2.0 * position
    row_scale = jnp.exp(jax.random.uniform(sub_keys[1], (SEQ,), jnp.float32, math.log(0.3), 0.0))
    col_scale = jnp.exp(jax.random.uniform(sub_keys[2], (C,), jnp.float32, math.log(0.5), math.log(2.0)))
    group_off = jax.random.normal(sub_keys[4], (GROUPS,), jnp.float32)
    offset_col = jnp.repeat(group_off, C // GROUPS) + 0.3 * jax.random.normal(sub_keys[3], (C,), jnp.float32)
    offset_rise = 0.3 + 2.7 * position
    drawn = offset_rise[:, None] * offset_col[None, :] + (rise_row * row_scale)[:, None] * col_scale[None, :] * noise_vals
    return jnp.clip(drawn, -40.0, 40.0).astype(jnp.bfloat16)


def draw_hint(key, part):
    sub_keys = [jax.random.fold_in(key, 41 + index) for index in range(6)]
    position = jnp.arange(SEQ, dtype=jnp.float32) / (SEQ - 1)
    sign_col = jnp.where(jax.random.bernoulli(sub_keys[0], 0.5, (C,)), 1.0, -1.0)
    ramp_size = jax.random.uniform(sub_keys[1], (C,), jnp.float32, 0.5, 1.5)
    offset_col = 1.5 * jax.random.normal(sub_keys[2], (C,), jnp.float32)
    noise_vals = jnp.clip(jax.random.normal(sub_keys[3], (SEQ, C), jnp.float32), -4.0, 4.0)
    ramp_amp = 2.5
    ramp = ramp_amp * (2.0 * position - 1.0)
    drawn = offset_col[None, :] + ramp[:, None] * (sign_col * ramp_size)[None, :] + noise_vals
    return jnp.clip(drawn, -6.0, 6.0).astype(jnp.bfloat16)


def weight_pair(key):
    base_key = jax.random.fold_in(key, 71)
    first_mat = jax.random.normal(jax.random.fold_in(base_key, 1), (C, C), jnp.float32)
    second_mat = jax.random.normal(jax.random.fold_in(base_key, 2), (C, C), jnp.float32)
    query_mat = first_mat * (1.5 / math.sqrt(C))
    key_mat = -(first_mat + 0.3 * second_mat) * (1.5 / math.sqrt(C))
    return (jnp.clip(query_mat, -2.0, 2.0), jnp.clip(key_mat, -2.0, 2.0))


def draw_query_weight(key, part):
    return weight_pair(key)[0].astype(jnp.bfloat16)


def draw_key_weight(key, part):
    return weight_pair(key)[1].astype(jnp.bfloat16)


def bell_draw(key, dims, scale, limit, kind=jnp.bfloat16):
    array = scale * jax.random.normal(key, dims, jnp.float32)
    return jnp.clip(array, min=-limit, max=limit).astype(kind)


def setup_inputs(seed: int = 0, part: int = 0) -> dict:
    keys = jax.random.split(jax.random.key(seed), 15)
    own_keys = jax.random.split(jax.random.fold_in(keys[14], part), 15)
    return {
        "features": draw_features(jax.random.fold_in(jax.random.fold_in(keys[14], part), 71), part),
        "hint": draw_hint(jax.random.fold_in(jax.random.fold_in(keys[14], part), 71), part),
        "conv_weight": bell_draw(keys[2], (3, 3, C, C), (9 * C) ** -0.5, 0.109375),
        "conv_bias": bell_draw(keys[3], (C,), 0.5, 3.0, jnp.float32),
        "zero_weight": bell_draw(keys[4], (C, C), C ** -0.5, 0.3125),
        "zero_bias": bell_draw(keys[5], (C,), 0.3, 2.0, jnp.float32),
        "group_gain": jnp.clip(1.0 + 0.1 * jax.random.normal(keys[6], (C,), jnp.float32), 0.5, 1.5),
        "proj_in": bell_draw(keys[7], (C, C), C ** -0.5, 0.3125),
        "norm_gain": jnp.clip(1.0 + 0.1 * jax.random.normal(keys[8], (C,), jnp.float32), 0.5, 1.5),
        "query_weight": draw_query_weight(jax.random.fold_in(keys[14], 71), part),
        "key_weight": draw_key_weight(jax.random.fold_in(keys[14], 71), part),
        "value_weight": bell_draw(keys[11], (C, C), C ** -0.5, 0.3125),
        "attn_out": bell_draw(keys[12], (C, C), C ** -0.5, 0.3125),
        "proj_out": bell_draw(keys[13], (C, C), C ** -0.5, 0.3125),
    }


norm_eps = 1e-06
layer_eps = 1e-05

def conv_extended(extended, conv_weight, conv_bias, width):
    line_count = extended.shape[0] // width - 2
    channels = extended.shape[1]
    lattice = extended.reshape(line_count + 2, width, channels)
    padded = jnp.pad(lattice, ((0, 0), (1, 1), (0, 0)))
    summed = jnp.zeros((line_count * width, conv_weight.shape[3]), jnp.float32)
    for row_shift in range(3):
        for col_shift in range(3):
            window = padded[row_shift:row_shift + line_count, col_shift:col_shift + width]
            window = window.reshape(line_count * width, channels)
            summed = summed + jnp.dot(window, conv_weight[row_shift, col_shift], preferred_element_type=jnp.float32)
    return summed + conv_bias

def control_merge(features, extended, conv_weight, conv_bias, zero_weight, zero_bias):
    control = jax.nn.silu(conv_extended(extended, conv_weight, conv_bias, WIDTH)).astype(jnp.bfloat16)
    branch = jnp.dot(control, zero_weight, preferred_element_type=jnp.float32) + zero_bias
    return (features.astype(jnp.float32) + branch).astype(jnp.bfloat16)

def group_apply(merged, mean_group, var_group, group_gain):
    per_group = merged.shape[1] // mean_group.shape[0]
    mean_chan = jnp.repeat(mean_group, per_group)
    inv_chan = jnp.repeat(lax.rsqrt(var_group + norm_eps), per_group)
    return ((merged.astype(jnp.float32) - mean_chan) * inv_chan * group_gain).astype(jnp.bfloat16)

def project_norm(grouped, proj_in, norm_gain):
    inner_rows = jnp.dot(grouped, proj_in, preferred_element_type=jnp.float32).astype(jnp.bfloat16)
    widened = inner_rows.astype(jnp.float32)
    centre = lax.optimization_barrier(jnp.mean(widened, axis=1, keepdims=True))
    spread = lax.optimization_barrier(jnp.mean(jnp.square(widened - centre), axis=1, keepdims=True))
    normed = ((widened - centre) * lax.rsqrt(spread + layer_eps) * norm_gain).astype(jnp.bfloat16)
    return (inner_rows, normed)

def reference(features, hint, conv_weight, conv_bias, zero_weight, zero_bias, group_gain, proj_in, norm_gain, query_weight, key_weight, value_weight, attn_out, proj_out):
    seq_len, channels = features.shape
    extended = jnp.pad(hint, ((WIDTH, WIDTH), (0, 0)))
    merged = control_merge(features, extended, conv_weight, conv_bias, zero_weight, zero_bias)
    widened = merged.astype(jnp.float32)
    per_group = channels // GROUPS
    entry_count = seq_len * per_group
    mean_group = lax.optimization_barrier(jnp.sum(widened.reshape(seq_len, GROUPS, per_group), axis=(0, 2))) / entry_count
    centred = widened - jnp.repeat(mean_group, per_group)
    var_group = lax.optimization_barrier(jnp.sum(jnp.square(centred).reshape(seq_len, GROUPS, per_group), axis=(0, 2))) / entry_count
    grouped = group_apply(merged, mean_group, var_group, group_gain)
    inner_rows, normed = project_norm(grouped, proj_in, norm_gain)
    head_dim = channels // HEADS

    def project(weight):
        made = jnp.dot(normed, weight, preferred_element_type=jnp.float32).astype(jnp.bfloat16)
        return made.reshape(seq_len, HEADS, head_dim)
    queries = project(query_weight)
    keys_wide = project(key_weight).astype(jnp.float32)
    values_wide = project(value_weight).astype(jnp.float32)
    block_len = math.gcd(seq_len, 512)
    score_scale = 1.0 / math.sqrt(head_dim)

    def attend(query_block):
        scores = jnp.einsum('qhd,khd->hqk', query_block.astype(jnp.float32), keys_wide) * score_scale
        row_max = lax.optimization_barrier(jnp.max(scores, axis=2, keepdims=True))
        weights = jnp.exp(scores - row_max)
        running_sum = lax.optimization_barrier(jnp.sum(weights, axis=2))
        rounded = lax.optimization_barrier(weights.astype(jnp.bfloat16)).astype(jnp.float32)
        weighted = jnp.einsum('hqk,khd->qhd', rounded, values_wide)
        return weighted / jnp.transpose(running_sum)[:, :, None]
    blocks = queries.reshape(seq_len // block_len, block_len, HEADS, head_dim)
    attended = lax.map(attend, blocks).reshape(seq_len, channels).astype(jnp.bfloat16)
    after_attn = (inner_rows.astype(jnp.float32) + jnp.dot(attended, attn_out, preferred_element_type=jnp.float32)).astype(jnp.bfloat16)
    return (merged.astype(jnp.float32) + jnp.dot(after_attn, proj_out, preferred_element_type=jnp.float32)).astype(jnp.bfloat16)
```

```python
import functools
import math

import jax
import jax.numpy as jnp
from jax import lax
from jax.experimental import pallas as pl
from jax.experimental.pallas import tpu as pltpu
from jax.sharding import Mesh
from jax.sharding import PartitionSpec as P

HEADS = 8
GROUPS = 32
WIDTH = 128
SEQ = ("x", "z", "c")
DP_SEQ = ("dp", "x", "z", "c")
NORM_EPS = 1e-06
LAYER_EPS = 1e-05
HIGHEST = lax.Precision.HIGHEST
F32 = jnp.float32
BF16 = jnp.bfloat16
VMEM = pl.BlockSpec(memory_space=pltpu.VMEM)
MIB = 1024 * 1024


def dot(a, b):
    return jnp.dot(a, b, preferred_element_type=F32)


def exact_dot(a, b):
    return jnp.dot(a, b, precision=HIGHEST, preferred_element_type=F32)


def call(body, out_shape, args, scratch=(), limit=24, flops=0, read=0, trans=0):
    many = isinstance(out_shape, (list, tuple))
    return pl.pallas_call(
        body,
        out_shape=out_shape,
        in_specs=[VMEM] * len(args),
        out_specs=[VMEM] * len(out_shape) if many else VMEM,
        scratch_shapes=scratch,
        compiler_params=pltpu.CompilerParams(vmem_limit_bytes=limit * MIB),
        cost_estimate=pl.CostEstimate(flops=flops, bytes_accessed=read, transcendentals=trans),
    )(*args)


def group_spread(channels, lanes, first):
    per_group = channels // GROUPS
    lane = lax.broadcasted_iota(jnp.int32, (lanes, channels), 0)
    chan = lax.broadcasted_iota(jnp.int32, (lanes, channels), 1)
    low = (lane - first) * per_group
    inside = (chan >= low) & (chan < low + per_group) & (lane >= first) & (lane < first + GROUPS)
    return inside.astype(F32)


def group_gather(channels, lanes, first):
    per_group = channels // GROUPS
    lane = lax.broadcasted_iota(jnp.int32, (channels, lanes), 1)
    chan = lax.broadcasted_iota(jnp.int32, (channels, lanes), 0)
    low = (lane - first) * per_group
    inside = (chan >= low) & (chan < low + per_group) & (lane >= first) & (lane < first + GROUPS)
    return inside.astype(F32)


def taps(row, weight, index):
    tokens, channels = row.shape
    wide = row.astype(F32)
    at = lax.broadcasted_iota(jnp.int32, (tokens, channels), 0)
    left = jnp.where(at == 0, 0.0, pltpu.roll(wide, 1, 0)).astype(BF16)
    right = jnp.where(at == tokens - 1, 0.0, pltpu.roll(wide, tokens - 1, 0)).astype(BF16)
    total = dot(left, weight[index, 0])
    total += dot(row, weight[index, 1])
    return total + dot(right, weight[index, 2])


def own_row_body(hint, weight, bias, out):
    out[...] = taps(hint[...], weight, 0) + bias[...]


def merge_body(partial, above, below, weight_up, weight_down, zero_weight, zero_bias, features, merged_out, stats_out):
    conv = partial[...] + taps(above[...], weight_up, 0) + taps(below[...], weight_down, 0)
    control = (conv / (1.0 + jnp.exp(-conv))).astype(BF16)
    branch = dot(control, zero_weight[...]) + zero_bias[...]
    merged = (features[...].astype(F32) + branch).astype(BF16)
    merged_out[...] = merged
    wide = merged.astype(F32)
    tokens, channels = wide.shape
    lanes = stats_out.shape[1]
    entries = tokens * (channels // GROUPS)
    mean = exact_dot(jnp.sum(wide, axis=0, keepdims=True), group_gather(channels, lanes, 0)) / entries
    centred = wide - exact_dot(mean, group_spread(channels, lanes, 0))
    square = exact_dot(
        jnp.sum(centred * centred, axis=0, keepdims=True), group_gather(channels, lanes, GROUPS)
    )
    stats_out[...] = jnp.broadcast_to(mean + square / entries, stats_out.shape)


def project_body(stats, merged, group_gain, proj_in, norm_gain, wq, wk, wv, inner_out, send):
    channels = merged.shape[1]
    lanes = stats.shape[1]
    head_dim = channels // HEADS
    everyone = stats[...]
    average = jnp.mean(everyone, axis=0, keepdims=True)
    between = jnp.mean(jnp.square(everyone - average), axis=0, keepdims=True)
    spread = group_spread(channels, lanes, 0)
    mean = exact_dot(average, spread)
    variance = exact_dot(average, group_spread(channels, lanes, GROUPS)) + exact_dot(between, spread)
    factor = lax.rsqrt(variance + NORM_EPS)
    grouped = ((merged[...].astype(F32) - mean) * factor * group_gain[...]).astype(BF16)
    inner = dot(grouped, proj_in[...]).astype(BF16)
    inner_out[...] = inner
    wide = inner.astype(F32)
    centred = wide - jnp.mean(wide, axis=1, keepdims=True)
    variance = jnp.mean(centred * centred, axis=1, keepdims=True)
    normed = (centred * lax.rsqrt(variance + LAYER_EPS) * norm_gain[...]).astype(BF16)
    scale = math.log2(math.e) / math.sqrt(head_dim)
    queries = (dot(normed, wq[...]) * scale).T
    keys = dot(normed, wk[...]).T
    values = dot(normed, wv[...]).T
    gap = jnp.zeros((send.shape[1] - 3 * head_dim, queries.shape[1]), F32)
    for h in range(HEADS):
        rows = slice(h * head_dim, (h + 1) * head_dim)
        block = jnp.concatenate([queries[rows], gap, keys[rows], values[rows]], axis=0)
        send[h] = block.astype(BF16)


def attend_body(head_dim, q_rows, first, last, *refs):
    received, refs = refs[0], refs[1:]
    if not first:
        acc_in, max_in, refs = refs[0], refs[1], refs[2:]
    outs = 1 if last else 2
    pieces, outs = refs[: len(refs) - outs], refs[len(refs) - outs :]
    blocks, _, tokens = received.shape
    depth = received.shape[1] - pieces[0].shape[1]
    per_step = q_rows // tokens

    def step(i, carry):
        rows = pl.ds(pl.multiple_of(i * q_rows, q_rows), q_rows)
        queries = jnp.concatenate(
            [received[i * per_step + j, :depth, :].astype(F32).T for j in range(per_step)], axis=0
        ).astype(BF16)
        if first:
            acc = top = None
        else:
            acc, top = acc_in[rows, :], max_in[rows, :1]
        for piece in pieces:
            pair = jnp.concatenate([piece[b] for b in range(piece.shape[0])], axis=1)
            scores = dot(queries, pair[:depth])
            high = jnp.max(scores, axis=1, keepdims=True)
            new_top = high if top is None else jnp.maximum(top, high)
            probs = jnp.exp2(scores - new_top).astype(BF16)
            ones = jnp.ones((128 - pair.shape[0], pair.shape[1]), BF16)
            product = lax.dot_general(
                probs,
                jnp.concatenate([pair, ones], axis=0),
                (((1,), (1,)), ((), ())),
                preferred_element_type=F32,
            )
            acc = product if acc is None else acc * jnp.exp2(top - new_top) + product
            top = new_top
        if last:
            total = acc.T
            result = total[head_dim : 2 * head_dim] / total[2 * head_dim : 2 * head_dim + 1]
            for j in range(per_step):
                outs[0][i * per_step + j] = result[:, j * tokens : (j + 1) * tokens].astype(BF16)
        else:
            outs[0][rows, :] = acc
            outs[1][rows, :] = jnp.broadcast_to(top, (q_rows, 128))
        return carry

    lax.fori_loop(0, blocks // per_step, step, 0)


def attend(received, pieces, state, last, head_dim, q_rows=512):
    blocks, _, tokens = received.shape
    args = [received, *(state or ()), *pieces]
    rows = blocks * tokens
    if last:
        out_shape = jax.ShapeDtypeStruct((blocks, head_dim, tokens), BF16)
    else:
        out_shape = [jax.ShapeDtypeStruct((rows, 128), F32)] * 2
    keys = sum(p.shape[0] * p.shape[2] for p in pieces)
    return call(
        functools.partial(attend_body, head_dim, q_rows, state is None, last),
        out_shape,
        args,
        limit=48,
        flops=2 * rows * keys * 512,
        read=keys * 160,
        trans=rows * keys,
    )


def finish_body(attended, inner, merged, attn_out, proj_out, out):
    rows = attended[...].astype(F32).T.astype(BF16)
    after = (inner[...].astype(F32) + dot(rows, attn_out[...])).astype(BF16)
    out[...] = (merged[...].astype(F32) + dot(after, proj_out[...])).astype(BF16)


def local(
    features,
    hint,
    conv_weight,
    conv_bias,
    zero_weight,
    zero_bias,
    group_gain,
    proj_in,
    norm_gain,
    query_weight,
    key_weight,
    value_weight,
    attn_out,
    proj_out,
):
    tokens, channels = features.shape
    head_dim = channels // HEADS
    everyone = lax.axis_size(SEQ)
    shape = jax.ShapeDtypeStruct
    onward = [(i, i + 1) for i in range(everyone - 1)]
    above = lax.ppermute(hint, SEQ, onward)
    below = lax.ppermute(hint, SEQ, [(b, a) for a, b in onward])
    row = lambda v: v.reshape(1, channels)
    partial = call(
        own_row_body,
        shape((tokens, channels), F32),
        (hint, conv_weight[1:2], row(conv_bias)),
        flops=2 * tokens * channels * channels * 3,
        read=3 * channels * channels * 2,
    )
    merged, stats = call(
        merge_body,
        [shape((tokens, channels), BF16), shape((everyone, 128), F32)],
        (partial, above, below, conv_weight[:1], conv_weight[2:], zero_weight, row(zero_bias), features),
        flops=2 * tokens * channels * channels * 7,
        read=7 * channels * channels * 2,
    )
    stats = lax.all_to_all(stats, SEQ, 0, 0, tiled=True)
    inner, send = call(
        project_body,
        [shape((tokens, channels), BF16), shape((HEADS, 128, tokens), BF16)],
        (stats, merged, row(group_gain), proj_in, row(norm_gain), query_weight, key_weight, value_weight),
        flops=2 * tokens * channels * channels * 4,
        read=4 * channels * channels * 2,
    )
    received = lax.all_to_all(send, "z", 0, 0, tiled=True)
    pair = received[:, 128 - 2 * head_dim :, :]
    by_core = lax.all_gather(pair, "c")
    by_chip = lax.all_gather(by_core, "x")
    pieces = [by_chip[i, j] for i in range(by_chip.shape[0]) for j in range(by_chip.shape[1])]
    result = attend(received, pieces, None, True, head_dim)
    attended = lax.all_to_all(result, "z", 0, 0, tiled=True).reshape(channels, tokens)
    return call(
        finish_body,
        shape((tokens, channels), BF16),
        (attended, inner, merged, attn_out, proj_out),
        flops=2 * tokens * channels * channels * 2,
        read=2 * channels * channels * 2,
    )


def solution(mesh):
    torus = Mesh(mesh.devices.reshape(mesh.shape["dp"], 4, 8, 2), DP_SEQ)
    return jax.shard_map(
        local,
        mesh=torus,
        in_specs=(P(DP_SEQ, None), P(DP_SEQ, None)) + (P(),) * 12,
        out_specs=P(DP_SEQ, None),
        check_vma=False,
    )
```

```python
import functools
import math

import jax
import jax.numpy as jnp
from jax import lax
from jax.experimental import pallas as pl
from jax.experimental.pallas import tpu as pltpu
from jax.sharding import Mesh
from jax.sharding import PartitionSpec as P

HEADS = 8
GROUPS = 32
WIDTH = 128
SEQ = ("x", "z", "c")
DP_SEQ = ("dp", "x", "z", "c")
NORM_EPS = 1e-06
LAYER_EPS = 1e-05
HIGHEST = lax.Precision.HIGHEST
F32 = jnp.float32
BF16 = jnp.bfloat16
VMEM = pl.BlockSpec(memory_space=pltpu.VMEM)
MIB = 1024 * 1024


def dot(a, b):
    return jnp.dot(a, b, preferred_element_type=F32)


def exact_dot(a, b):
    return jnp.dot(a, b, precision=HIGHEST, preferred_element_type=F32)


def call(body, out_shape, args, scratch=(), limit=24, flops=0, read=0, trans=0):
    many = isinstance(out_shape, (list, tuple))
    return pl.pallas_call(
        body,
        out_shape=out_shape,
        in_specs=[VMEM] * len(args),
        out_specs=[VMEM] * len(out_shape) if many else VMEM,
        scratch_shapes=scratch,
        compiler_params=pltpu.CompilerParams(vmem_limit_bytes=limit * MIB),
        cost_estimate=pl.CostEstimate(flops=flops, bytes_accessed=read, transcendentals=trans),
    )(*args)


def group_spread(channels, lanes, first):
    per_group = channels // GROUPS
    lane = lax.broadcasted_iota(jnp.int32, (lanes, channels), 0)
    chan = lax.broadcasted_iota(jnp.int32, (lanes, channels), 1)
    low = (lane - first) * per_group
    inside = (chan >= low) & (chan < low + per_group) & (lane >= first) & (lane < first + GROUPS)
    return inside.astype(F32)


def group_gather(channels, lanes, first):
    per_group = channels // GROUPS
    lane = lax.broadcasted_iota(jnp.int32, (channels, lanes), 1)
    chan = lax.broadcasted_iota(jnp.int32, (channels, lanes), 0)
    low = (lane - first) * per_group
    inside = (chan >= low) & (chan < low + per_group) & (lane >= first) & (lane < first + GROUPS)
    return inside.astype(F32)


def turned(ref):
    return ref[...].astype(F32).T


def taps(wide, weight, index):
    tokens, channels = wide.shape
    at = lax.broadcasted_iota(jnp.int32, (tokens, channels), 0)
    left = jnp.where(at == 0, 0.0, pltpu.roll(wide, 1, 0)).astype(BF16)
    right = jnp.where(at == tokens - 1, 0.0, pltpu.roll(wide, tokens - 1, 0)).astype(BF16)
    total = dot(left, weight[index, 0])
    total += dot(wide.astype(BF16), weight[index, 1])
    return total + dot(right, weight[index, 2])


def own_row_body(hint, weight, bias, out):
    out[...] = taps(turned(hint), weight, 1) + bias[...]


def merge_body(partial, above, below, weight, zero_weight, zero_bias, features, merged_out, stats_out):
    conv = partial[...] + taps(turned(above), weight, 0) + taps(turned(below), weight, 2)
    control = (conv / (1.0 + jnp.exp(-conv))).astype(BF16)
    branch = dot(control, zero_weight[...]) + zero_bias[...]
    merged = (turned(features) + branch).astype(BF16)
    merged_out[...] = merged
    wide = merged.astype(F32)
    tokens, channels = wide.shape
    lanes = stats_out.shape[1]
    entries = tokens * (channels // GROUPS)
    mean = exact_dot(jnp.sum(wide, axis=0, keepdims=True), group_gather(channels, lanes, 0)) / entries
    centred = wide - exact_dot(mean, group_spread(channels, lanes, 0))
    square = exact_dot(
        jnp.sum(centred * centred, axis=0, keepdims=True), group_gather(channels, lanes, GROUPS)
    )
    stats_out[...] = jnp.broadcast_to(mean + square / entries, stats_out.shape)


def project_body(stats, merged, group_gain, proj_in, norm_gain, wq, wk, wv, inner_out, send):
    channels = merged.shape[1]
    lanes = stats.shape[1]
    head_dim = channels // HEADS
    everyone = stats[...]
    average = jnp.mean(everyone, axis=0, keepdims=True)
    between = jnp.mean(jnp.square(everyone - average), axis=0, keepdims=True)
    spread = group_spread(channels, lanes, 0)
    mean = exact_dot(average, spread)
    variance = exact_dot(average, group_spread(channels, lanes, GROUPS)) + exact_dot(between, spread)
    factor = lax.rsqrt(variance + NORM_EPS)
    grouped = ((merged[...].astype(F32) - mean) * factor * group_gain[...]).astype(BF16)
    inner = dot(grouped, proj_in[...]).astype(BF16)
    inner_out[...] = inner
    wide = inner.astype(F32)
    centred = wide - jnp.mean(wide, axis=1, keepdims=True)
    variance = jnp.mean(centred * centred, axis=1, keepdims=True)
    normed = (centred * lax.rsqrt(variance + LAYER_EPS) * norm_gain[...]).astype(BF16)
    scale = math.log2(math.e) / math.sqrt(head_dim)
    queries = (dot(normed, wq[...]) * scale).T
    keys = dot(normed, wk[...]).T
    values = dot(normed, wv[...]).T
    gap = jnp.zeros((send.shape[1] - 3 * head_dim, queries.shape[1]), F32)
    for h in range(HEADS):
        rows = slice(h * head_dim, (h + 1) * head_dim)
        block = jnp.concatenate([queries[rows], gap, keys[rows], values[rows]], axis=0)
        send[h] = block.astype(BF16)


def attend_body(head_dim, q_rows, first, compact, n_queries, n_pieces, *refs):
    query_refs, refs = refs[:n_queries], refs[n_queries:]
    pieces, refs = refs[:n_pieces], refs[n_pieces:]
    if not first:
        states, refs = refs[: 2 * n_queries], refs[2 * n_queries :]
    blocks, depth, tokens = query_refs[0].shape
    per_step = q_rows // tokens

    def step(i, carry):
        rows = pl.ds(pl.multiple_of(i * q_rows, q_rows), q_rows)
        for n, received in enumerate(query_refs):
            queries = jnp.concatenate(
                [received[i * per_step + j].astype(F32).T for j in range(per_step)], axis=0
            ).astype(BF16)
            if first:
                acc = top = None
            else:
                acc, top = states[2 * n][rows, :], states[2 * n + 1][rows, :1]
            for piece in pieces:
                pair = jnp.concatenate([piece[b] for b in range(piece.shape[0])], axis=1)
                scores = dot(queries, pair[:depth])
                high = jnp.max(scores, axis=1, keepdims=True)
                new_top = high if top is None else jnp.maximum(top, high)
                probs = jnp.exp2(scores - new_top).astype(BF16)
                ones = jnp.ones((128 - pair.shape[0], pair.shape[1]), BF16)
                product = lax.dot_general(
                    probs,
                    jnp.concatenate([pair, ones], axis=0),
                    (((1,), (1,)), ((), ())),
                    preferred_element_type=F32,
                )
                acc = product if acc is None else acc * jnp.exp2(top - new_top) + product
                top = new_top
            if compact:
                both = acc.T[head_dim : 2 * head_dim + 8]
                tops = jnp.broadcast_to(top, (q_rows, 128)).T[:8]
                for j in range(per_step):
                    at = slice(j * tokens, (j + 1) * tokens)
                    refs[n][i * per_step + j, : head_dim + 8] = both[:, at]
                    refs[n][i * per_step + j, head_dim + 8 :] = tops[:, at]
            else:
                refs[2 * n][rows, :] = acc
                refs[2 * n + 1][rows, :] = jnp.broadcast_to(top, (q_rows, 128))
        return carry

    lax.fori_loop(0, blocks // per_step, step, 0)


def attend(queries, pieces, states, compact, head_dim, q_rows=512):
    blocks, _, tokens = queries[0].shape
    rows = blocks * tokens
    if compact:
        out_shape = [jax.ShapeDtypeStruct((blocks, head_dim + 16, tokens), F32)] * len(queries)
    else:
        out_shape = [jax.ShapeDtypeStruct((rows, 128), F32)] * (2 * len(queries))
    keys = sum(p.shape[0] * p.shape[2] for p in pieces) * len(queries)
    return call(
        functools.partial(
            attend_body, head_dim, q_rows, states is None, compact, len(queries), len(pieces)
        ),
        out_shape,
        [*queries, *pieces, *(states or ())],
        limit=48,
        flops=2 * rows * keys * 512,
        read=keys * 160,
        trans=rows * keys,
    )


def combine_body(head_dim, mine, theirs, out):
    a, b = mine[...], theirs[...]
    a_top, b_top = a[:, head_dim + 8 : head_dim + 9], b[:, head_dim + 8 : head_dim + 9]
    top = jnp.maximum(a_top, b_top)
    both = a[:, : head_dim + 8] * jnp.exp2(a_top - top) + b[:, : head_dim + 8] * jnp.exp2(b_top - top)
    out[...] = (both[:, :head_dim] / both[:, head_dim : head_dim + 1]).astype(BF16)


def finish_body(attended, inner, merged, attn_out, proj_out, out):
    rows = turned(attended).astype(BF16)
    after = (inner[...].astype(F32) + dot(rows, attn_out[...])).astype(BF16)
    out[...] = (merged[...].astype(F32) + dot(after, proj_out[...])).T.astype(BF16)


def local(
    features,
    hint,
    conv_weight,
    conv_bias,
    zero_weight,
    zero_bias,
    group_gain,
    proj_in,
    norm_gain,
    query_weight,
    key_weight,
    value_weight,
    attn_out,
    proj_out,
):
    tokens, channels = features.shape
    head_dim = channels // HEADS
    everyone = lax.axis_size(SEQ)
    shape = jax.ShapeDtypeStruct
    onward = [(i, i + 1) for i in range(everyone - 1)]
    hint, features = hint.T, features.T
    above = lax.ppermute(hint, SEQ, onward)
    below = lax.ppermute(hint, SEQ, [(b, a) for a, b in onward])
    row = lambda v: v.reshape(1, channels)
    partial = call(
        own_row_body,
        shape((tokens, channels), F32),
        (hint, conv_weight, row(conv_bias)),
        flops=2 * tokens * channels * channels * 3,
        read=9 * channels * channels * 2,
    )
    merged, stats = call(
        merge_body,
        [shape((tokens, channels), BF16), shape((everyone, 128), F32)],
        (partial, above, below, conv_weight, zero_weight, row(zero_bias), features),
        flops=2 * tokens * channels * channels * 7,
        read=7 * channels * channels * 2,
    )
    stats = lax.all_to_all(stats, SEQ, 0, 0, tiled=True)
    inner, send = call(
        project_body,
        [shape((tokens, channels), BF16), shape((HEADS, 128, tokens), BF16)],
        (stats, merged, row(group_gain), proj_in, row(norm_gain), query_weight, key_weight, value_weight),
        flops=2 * tokens * channels * channels * 4,
        read=4 * channels * channels * 2,
    )
    received = lax.all_to_all(send, "z", 0, 0, tiled=True)
    depth = 128 - 2 * head_dim
    queries, pair = received[:, :depth, :], received[:, depth:, :]
    swap = [(0, 1), (1, 0)]
    chips = lax.axis_size("x")
    ring = lambda by: [(i, (i + by) % chips) for i in range(chips)]
    others = lax.ppermute(queries, "c", swap)
    left, right, far = (lax.ppermute(pair, "x", ring(by)) for by in (1, chips - 1, 2))
    mine = attend([queries], [pair], None, False, head_dim)
    theirs = attend([others], [pair], None, False, head_dim)
    states = attend([queries, others], [left, right], [*mine, *theirs], False, head_dim)
    (theirs,) = attend([others], [far], states[2:], True, head_dim)
    back = lax.ppermute(theirs, "c", swap)
    (mine,) = attend([queries], [far], states[:2], True, head_dim)
    result = call(
        functools.partial(combine_body, head_dim), shape((HEADS, head_dim, tokens), BF16), (mine, back)
    )
    attended = lax.all_to_all(result, "z", 0, 0, tiled=True).reshape(channels, tokens)
    return call(
        finish_body,
        shape((channels, tokens), BF16),
        (attended, inner, merged, attn_out, proj_out),
        flops=2 * tokens * channels * channels * 2,
        read=2 * channels * channels * 2,
    ).T


def solution(mesh):
    torus = Mesh(mesh.devices.reshape(mesh.shape["dp"], 4, 8, 2), DP_SEQ)
    return jax.shard_map(
        local,
        mesh=torus,
        in_specs=(P(DP_SEQ, None), P(DP_SEQ, None)) + (P(),) * 12,
        out_specs=P(DP_SEQ, None),
        check_vma=False,
    )
```

```python
import functools
import math

import jax
import jax.numpy as jnp
from jax import lax
from jax.experimental import pallas as pl
from jax.experimental.pallas import tpu as pltpu
from jax.sharding import Mesh
from jax.sharding import PartitionSpec as P

HEADS = 8
GROUPS = 32
WIDTH = 128
SEQ = ("x", "z", "c")
DP_SEQ = ("dp", "x", "z", "c")
NORM_EPS = 1e-06
LAYER_EPS = 1e-05
HIGHEST = lax.Precision.HIGHEST
F32 = jnp.float32
BF16 = jnp.bfloat16
VMEM = pl.BlockSpec(memory_space=pltpu.VMEM)
SMEM = pl.BlockSpec(memory_space=pltpu.SMEM)
MIB = 1024 * 1024


def dot(a, b):
    return jnp.dot(a, b, preferred_element_type=F32)


def exact_dot(a, b):
    return jnp.dot(a, b, precision=HIGHEST, preferred_element_type=F32)


def call(body, out_shape, args, scratch=(), limit=24, flops=0, read=0, trans=0, smem=0):
    many = isinstance(out_shape, (list, tuple))
    return pl.pallas_call(
        body,
        out_shape=out_shape,
        in_specs=[SMEM] * smem + [VMEM] * (len(args) - smem),
        out_specs=[VMEM] * len(out_shape) if many else VMEM,
        scratch_shapes=scratch,
        compiler_params=pltpu.CompilerParams(vmem_limit_bytes=limit * MIB),
        cost_estimate=pl.CostEstimate(flops=flops, bytes_accessed=read, transcendentals=trans),
    )(*args)


def group_spread(channels, lanes, first):
    per_group = channels // GROUPS
    lane = lax.broadcasted_iota(jnp.int32, (lanes, channels), 0)
    chan = lax.broadcasted_iota(jnp.int32, (lanes, channels), 1)
    low = (lane - first) * per_group
    inside = (chan >= low) & (chan < low + per_group) & (lane >= first) & (lane < first + GROUPS)
    return inside.astype(F32)


def group_gather(channels, lanes, first):
    per_group = channels // GROUPS
    lane = lax.broadcasted_iota(jnp.int32, (channels, lanes), 1)
    chan = lax.broadcasted_iota(jnp.int32, (channels, lanes), 0)
    low = (lane - first) * per_group
    inside = (chan >= low) & (chan < low + per_group) & (lane >= first) & (lane < first + GROUPS)
    return inside.astype(F32)


def turned(ref):
    return ref[...].astype(F32).T


def taps(wide, weight, index):
    tokens, channels = wide.shape
    column = lax.broadcasted_iota(jnp.int32, (tokens, channels), 0)
    left = jnp.where(column == 0, 0.0, pltpu.roll(wide, 1, 0)).astype(BF16)
    right = jnp.where(column == tokens - 1, 0.0, pltpu.roll(wide, tokens - 1, 0)).astype(BF16)
    at = (lambda b: b) if index is None else (lambda b: (index, b))
    total = dot(left, weight[at(0)])
    total += dot(wide.astype(BF16), weight[at(1)])
    return total + dot(right, weight[at(2)])


def own_row_body(core, hint, pair, weight, bias, features, zero_weight, partial, odd_weight, features_out, zero_out):
    pair_row = 2 - 2 * core[0]
    partial[...] = taps(turned(hint), weight, 1) + taps(turned(pair), weight, pair_row) + bias[...]
    odd_weight[...] = weight[2 - pair_row]
    features_out[...] = turned(features)
    zero_out[...] = zero_weight[...]


def merge_body(partial, odd, odd_weight, zero_weight, zero_bias, features, merged_out, stats_out):
    conv = partial[...] + taps(turned(odd), odd_weight, None)
    control = (conv / (1.0 + jnp.exp(-conv))).astype(BF16)
    branch = dot(control, zero_weight[...]) + zero_bias[...]
    merged = (features[...] + branch).astype(BF16)
    merged_out[...] = merged
    wide = merged.astype(F32)
    tokens, channels = wide.shape
    lanes = stats_out.shape[1]
    entries = tokens * (channels // GROUPS)
    mean = exact_dot(jnp.sum(wide, axis=0, keepdims=True), group_gather(channels, lanes, 0)) / entries
    centred = wide - exact_dot(mean, group_spread(channels, lanes, 0))
    square = exact_dot(
        jnp.sum(centred * centred, axis=0, keepdims=True), group_gather(channels, lanes, GROUPS)
    )
    stats_out[...] = jnp.broadcast_to(mean + square / entries, stats_out.shape)


def project_body(stats, merged, group_gain, proj_in, norm_gain, wq, wk, wv, inner_out, send):
    channels = merged.shape[1]
    lanes = stats.shape[1]
    head_dim = channels // HEADS
    everyone = stats[...]
    average = jnp.mean(everyone, axis=0, keepdims=True)
    between = jnp.mean(jnp.square(everyone - average), axis=0, keepdims=True)
    spread = group_spread(channels, lanes, 0)
    mean = exact_dot(average, spread)
    variance = exact_dot(average, group_spread(channels, lanes, GROUPS)) + exact_dot(between, spread)
    factor = lax.rsqrt(variance + NORM_EPS)
    grouped = ((merged[...].astype(F32) - mean) * factor * group_gain[...]).astype(BF16)
    inner = dot(grouped, proj_in[...]).astype(BF16)
    inner_out[...] = inner
    wide = inner.astype(F32)
    centred = wide - jnp.mean(wide, axis=1, keepdims=True)
    variance = jnp.mean(centred * centred, axis=1, keepdims=True)
    normed = (centred * lax.rsqrt(variance + LAYER_EPS) * norm_gain[...]).astype(BF16)
    scale = math.log2(math.e) / math.sqrt(head_dim)
    queries = (dot(normed, wq[...]) * scale).T
    keys = dot(normed, wk[...]).T
    values = dot(normed, wv[...]).T
    gap = jnp.zeros((send.shape[1] - 3 * head_dim, queries.shape[1]), F32)
    for h in range(HEADS):
        rows = slice(h * head_dim, (h + 1) * head_dim)
        block = jnp.concatenate([queries[rows], gap, keys[rows], values[rows]], axis=0)
        send[h] = block.astype(BF16)


def attend_body(head_dim, q_rows, first, compact, n_queries, n_pieces, *refs):
    query_refs, refs = refs[:n_queries], refs[n_queries:]
    pieces, refs = refs[:n_pieces], refs[n_pieces:]
    if not first:
        states, refs = refs[: 2 * n_queries], refs[2 * n_queries :]
    blocks, depth, tokens = query_refs[0].shape
    per_step = q_rows // tokens

    for i in range(blocks // per_step):
        rows = slice(i * q_rows, (i + 1) * q_rows)
        for n, received in enumerate(query_refs):
            queries = jnp.concatenate(
                [received[i * per_step + j].astype(F32).T for j in range(per_step)], axis=0
            ).astype(BF16)
            if first:
                acc = top = None
            else:
                acc, top = states[2 * n][rows, :], states[2 * n + 1][rows, :1]
            for piece in pieces:
                pair = jnp.concatenate([piece[b] for b in range(piece.shape[0])], axis=1)
                scores = dot(queries, pair[:depth])
                high = jnp.max(scores, axis=1, keepdims=True)
                new_top = high if top is None else jnp.maximum(top, high)
                probs = jnp.exp2(scores - new_top).astype(BF16)
                ones = jnp.ones((128 - pair.shape[0], pair.shape[1]), BF16)
                product = lax.dot_general(
                    probs,
                    jnp.concatenate([pair, ones], axis=0),
                    (((1,), (1,)), ((), ())),
                    preferred_element_type=F32,
                )
                acc = product if acc is None else acc * jnp.exp2(top - new_top) + product
                top = new_top
            if compact:
                both = acc.T[head_dim : 2 * head_dim + 8]
                tops = jnp.broadcast_to(top, (q_rows, 128)).T[:8]
                for j in range(per_step):
                    at = slice(j * tokens, (j + 1) * tokens)
                    refs[n][i * per_step + j, : head_dim + 8] = both[:, at]
                    refs[n][i * per_step + j, head_dim + 8 :] = tops[:, at]
            else:
                refs[2 * n][rows, :] = acc
                refs[2 * n + 1][rows, :] = jnp.broadcast_to(top, (q_rows, 128))


def attend(queries, pieces, states, compact, head_dim, q_rows=1024):
    blocks, _, tokens = queries[0].shape
    rows = blocks * tokens
    if compact:
        out_shape = [jax.ShapeDtypeStruct((blocks, head_dim + 16, tokens), F32)] * len(queries)
    else:
        out_shape = [jax.ShapeDtypeStruct((rows, 128), F32)] * (2 * len(queries))
    keys = sum(p.shape[0] * p.shape[2] for p in pieces) * len(queries)
    return call(
        functools.partial(
            attend_body, head_dim, q_rows, states is None, compact, len(queries), len(pieces)
        ),
        out_shape,
        [*queries, *pieces, *(states or ())],
        limit=48,
        flops=2 * rows * keys * 512,
        read=keys * 160,
        trans=rows * keys,
    )


def combine_body(head_dim, mine, theirs, out):
    a, b = mine[...], theirs[...]
    a_top, b_top = a[:, head_dim + 8 : head_dim + 9], b[:, head_dim + 8 : head_dim + 9]
    top = jnp.maximum(a_top, b_top)
    both = a[:, : head_dim + 8] * jnp.exp2(a_top - top) + b[:, : head_dim + 8] * jnp.exp2(b_top - top)
    out[...] = (both[:, :head_dim] / both[:, head_dim : head_dim + 1]).astype(BF16)


def finish_body(attended, inner, merged, attn_out, proj_out, out):
    rows = turned(attended).astype(BF16)
    after = (inner[...].astype(F32) + dot(rows, attn_out[...])).astype(BF16)
    out[...] = (merged[...].astype(F32) + dot(after, proj_out[...])).T.astype(BF16)


def local(
    features,
    hint,
    conv_weight,
    conv_bias,
    zero_weight,
    zero_bias,
    group_gain,
    proj_in,
    norm_gain,
    query_weight,
    key_weight,
    value_weight,
    attn_out,
    proj_out,
):
    tokens, channels = features.shape
    head_dim = channels // HEADS
    everyone = lax.axis_size(SEQ)
    shape = jax.ShapeDtypeStruct
    hint, features = hint.T, features.T
    core = lax.axis_index("c").reshape(1)
    swap = [(0, 1), (1, 0)]
    ends = [(i, i + 1) for i in range(1, everyone - 1, 2)]
    odd = lax.ppermute(hint, SEQ, ends + [(b, a) for a, b in ends])
    pair = lax.ppermute(hint, "c", swap)
    row = lambda v: v.reshape(1, channels)
    partial, odd_weight, features, zero_weight = call(
        own_row_body,
        [
            shape((tokens, channels), F32),
            shape(conv_weight.shape[1:], BF16),
            shape((tokens, channels), F32),
            shape(zero_weight.shape, BF16),
        ],
        (core, hint, pair, conv_weight, row(conv_bias), features, zero_weight),
        smem=1,
        flops=2 * tokens * channels * channels * 6,
        read=10 * channels * channels * 2,
    )
    merged, stats = call(
        merge_body,
        [shape((tokens, channels), BF16), shape((everyone, 128), F32)],
        (partial, odd, odd_weight, zero_weight, row(zero_bias), features),
        flops=2 * tokens * channels * channels * 4,
        read=4 * channels * channels * 2,
    )
    stats = lax.all_to_all(stats, SEQ, 0, 0, tiled=True)
    inner, send = call(
        project_body,
        [shape((tokens, channels), BF16), shape((HEADS, 128, tokens), BF16)],
        (stats, merged, row(group_gain), proj_in, row(norm_gain), query_weight, key_weight, value_weight),
        flops=2 * tokens * channels * channels * 4,
        read=4 * channels * channels * 2,
    )
    received = lax.all_to_all(send, "z", 0, 0, tiled=True)
    depth = 128 - 2 * head_dim
    queries, pair = received[:, :depth, :], received[:, depth:, :]
    chips = lax.axis_size("x")
    ring = lambda by: [(i, (i + by) % chips) for i in range(chips)]
    others = lax.ppermute(queries, "c", swap)
    pieces = [lax.ppermute(pair, "x", ring(by)) for by in (1, chips - 1, 2)]
    states = attend([queries, others], [pair], None, False, head_dim)
    (theirs,) = attend([others], pieces, states[2:], True, head_dim)
    back = lax.ppermute(theirs, "c", swap)
    (mine,) = attend([queries], pieces, states[:2], True, head_dim)
    result = call(
        functools.partial(combine_body, head_dim), shape((HEADS, head_dim, tokens), BF16), (mine, back)
    )
    attended = lax.all_to_all(result, "z", 0, 0, tiled=True).reshape(channels, tokens)
    return call(
        finish_body,
        shape((channels, tokens), BF16),
        (attended, inner, merged, attn_out, proj_out),
        flops=2 * tokens * channels * channels * 2,
        read=2 * channels * channels * 2,
    ).T


def solution(mesh):
    torus = Mesh(mesh.devices.reshape(mesh.shape["dp"], 4, 8, 2), DP_SEQ)
    return jax.shard_map(
        local,
        mesh=torus,
        in_specs=(P(DP_SEQ, None), P(DP_SEQ, None)) + (P(),) * 12,
        out_specs=P(DP_SEQ, None),
        check_vma=False,
    )
```

```python
import functools
import math

import jax
import jax.numpy as jnp
from jax import lax
from jax.experimental import pallas as pl
from jax.experimental.pallas import tpu as pltpu
from jax.sharding import Mesh
from jax.sharding import PartitionSpec as P

HEADS = 8
GROUPS = 32
WIDTH = 128
SEQ = ("x", "z", "c")
DP_SEQ = ("dp", "x", "z", "c")
NORM_EPS = 1e-06
LAYER_EPS = 1e-05
HIGHEST = lax.Precision.HIGHEST
F32 = jnp.float32
BF16 = jnp.bfloat16
VMEM = pl.BlockSpec(memory_space=pltpu.VMEM)
SMEM = pl.BlockSpec(memory_space=pltpu.SMEM)
AWAY = pl.BlockSpec(memory_space=pltpu.HBM)
MIB = 1024 * 1024


def dot(a, b):
    return jnp.dot(a, b, preferred_element_type=F32)


def exact_dot(a, b):
    return jnp.dot(a, b, precision=HIGHEST, preferred_element_type=F32)


def call(body, out_shape, args, scratch=(), limit=24, flops=0, read=0, trans=0, smem=0, away=0):
    many = isinstance(out_shape, (list, tuple))
    return pl.pallas_call(
        body,
        out_shape=out_shape,
        in_specs=[SMEM] * smem + [VMEM] * (len(args) - smem - away) + [AWAY] * away,
        out_specs=[VMEM] * len(out_shape) if many else VMEM,
        scratch_shapes=scratch,
        compiler_params=pltpu.CompilerParams(vmem_limit_bytes=limit * MIB),
        cost_estimate=pl.CostEstimate(flops=flops, bytes_accessed=read, transcendentals=trans),
    )(*args)


def group_spread(channels, lanes, first):
    per_group = channels // GROUPS
    lane = lax.broadcasted_iota(jnp.int32, (lanes, channels), 0)
    chan = lax.broadcasted_iota(jnp.int32, (lanes, channels), 1)
    low = (lane - first) * per_group
    inside = (chan >= low) & (chan < low + per_group) & (lane >= first) & (lane < first + GROUPS)
    return inside.astype(F32)


def group_gather(channels, lanes, first):
    per_group = channels // GROUPS
    lane = lax.broadcasted_iota(jnp.int32, (channels, lanes), 1)
    chan = lax.broadcasted_iota(jnp.int32, (channels, lanes), 0)
    low = (lane - first) * per_group
    inside = (chan >= low) & (chan < low + per_group) & (lane >= first) & (lane < first + GROUPS)
    return inside.astype(F32)


def turned(ref):
    return ref[...].astype(F32).T


def taps(wide, weight, index):
    tokens, channels = wide.shape
    column = lax.broadcasted_iota(jnp.int32, (tokens, channels), 0)
    left = jnp.where(column == 0, 0.0, pltpu.roll(wide, 1, 0)).astype(BF16)
    right = jnp.where(column == tokens - 1, 0.0, pltpu.roll(wide, tokens - 1, 0)).astype(BF16)
    at = (lambda b: b) if index is None else (lambda b: (index, b))
    total = dot(left, weight[at(0)])
    total += dot(wide.astype(BF16), weight[at(1)])
    return total + dot(right, weight[at(2)])


def own_row_body(
    core, pair, conv_bias, zero_bias, group_gain, norm_gain, hint, weight, features, zero_weight,
    partial, odd_weight, features_out, zero_out, bias_out, group_out, norm_out,
    hint_here, weight_here, features_here, sems,
):
    pair_row = 2 - 2 * core[0]
    copies = [
        pltpu.make_async_copy(source, target, sems.at[i])
        for i, (source, target) in enumerate(
            (
                (hint, hint_here),
                (weight.at[1], weight_here.at[0]),
                (weight.at[pair_row], weight_here.at[1]),
                (features, features_here),
                (zero_weight, zero_out),
                (weight.at[2 - pair_row], odd_weight),
            )
        )
    ]
    for copy in copies:
        copy.start()
    width = conv_bias.shape[0]
    bias_out[...] = zero_bias[...].reshape(1, width)
    group_out[...] = group_gain[...].reshape(1, width)
    norm_out[...] = norm_gain[...].reshape(1, width)
    copies[0].wait()
    copies[1].wait()
    total = taps(turned(hint_here), weight_here, 0) + conv_bias[...].reshape(1, width)
    copies[2].wait()
    partial[...] = total + taps(turned(pair), weight_here, 1)
    copies[3].wait()
    features_out[...] = turned(features_here)
    copies[4].wait()
    copies[5].wait()


def merge_body(partial, odd, odd_weight, zero_weight, zero_bias, features, merged_out, stats_out):
    conv = partial[...] + taps(turned(odd), odd_weight, None)
    control = (conv / (1.0 + jnp.exp(-conv))).astype(BF16)
    branch = dot(control, zero_weight[...]) + zero_bias[...]
    merged = (features[...] + branch).astype(BF16)
    merged_out[...] = merged
    wide = merged.astype(F32)
    tokens, channels = wide.shape
    lanes = stats_out.shape[1]
    entries = tokens * (channels // GROUPS)
    mean = exact_dot(jnp.sum(wide, axis=0, keepdims=True), group_gather(channels, lanes, 0)) / entries
    centred = wide - exact_dot(mean, group_spread(channels, lanes, 0))
    square = exact_dot(
        jnp.sum(centred * centred, axis=0, keepdims=True), group_gather(channels, lanes, GROUPS)
    )
    stats_out[...] = jnp.broadcast_to(mean + square / entries, stats_out.shape)


def project_body(stats, merged, group_gain, proj_in, norm_gain, wq, wk, wv, inner_out, send):
    channels = merged.shape[1]
    lanes = stats.shape[1]
    head_dim = channels // HEADS
    everyone = stats[...]
    average = jnp.mean(everyone, axis=0, keepdims=True)
    between = jnp.mean(jnp.square(everyone - average), axis=0, keepdims=True)
    spread = group_spread(channels, lanes, 0)
    mean = exact_dot(average, spread)
    variance = exact_dot(average, group_spread(channels, lanes, GROUPS)) + exact_dot(between, spread)
    factor = lax.rsqrt(variance + NORM_EPS)
    grouped = ((merged[...].astype(F32) - mean) * factor * group_gain[...]).astype(BF16)
    inner = dot(grouped, proj_in[...]).astype(BF16)
    inner_out[...] = inner
    wide = inner.astype(F32)
    centred = wide - jnp.mean(wide, axis=1, keepdims=True)
    variance = jnp.mean(centred * centred, axis=1, keepdims=True)
    normed = (centred * lax.rsqrt(variance + LAYER_EPS) * norm_gain[...]).astype(BF16)
    scale = math.log2(math.e) / math.sqrt(head_dim)
    queries = (dot(normed, wq[...]) * scale).T
    keys = dot(normed, wk[...]).T
    values = dot(normed, wv[...]).T
    gap = jnp.zeros((send.shape[1] - 3 * head_dim, queries.shape[1]), F32)
    for h in range(HEADS):
        rows = slice(h * head_dim, (h + 1) * head_dim)
        block = jnp.concatenate([queries[rows], gap, keys[rows], values[rows]], axis=0)
        send[h] = block.astype(BF16)


def attend_body(head_dim, first, n_queries, n_pieces, *refs):
    query_refs, refs = refs[:n_queries], refs[n_queries:]
    pieces, refs = refs[:n_pieces], refs[n_pieces:]
    if not first:
        states, refs = refs[:n_queries], refs[n_queries:]
    depth = query_refs[0].shape[1]
    side_by_side = lambda ref: jnp.concatenate([ref[b] for b in range(ref.shape[0])], axis=1)
    pairs = [side_by_side(piece) for piece in pieces]
    keys = [pair[:depth].astype(F32).T.astype(BF16) for pair in pairs]
    ones = jnp.ones((16, pairs[0].shape[1]), BF16)
    summed = jnp.concatenate([jnp.concatenate([pair, ones], axis=0) for pair in pairs], axis=1)
    rows = summed.shape[0] - head_dim
    for n, query_ref in enumerate(query_refs):
        queries = side_by_side(query_ref)
        scores = [dot(k, queries) for k in keys]
        top = functools.reduce(jnp.maximum, [jnp.max(s, axis=0, keepdims=True) for s in scores])
        if not first:
            before = states[n][rows : rows + 1, :]
            top = jnp.maximum(top, before)
        probs = jnp.concatenate([jnp.exp2(s - top).astype(BF16) for s in scores], axis=0)
        total = dot(summed, probs)[head_dim:]
        if not first:
            total += states[n][:rows, :] * jnp.exp2(before - top)
        refs[n][:rows, :] = total
        refs[n][rows:, :] = jnp.broadcast_to(top, (8, top.shape[1]))


def attend(queries, pieces, states, head_dim):
    blocks, _, tokens = queries[0].shape
    columns = blocks * tokens
    keys = sum(p.shape[0] * p.shape[2] for p in pieces) * len(queries)
    return call(
        functools.partial(attend_body, head_dim, states is None, len(queries), len(pieces)),
        [jax.ShapeDtypeStruct((head_dim + 24, columns), F32)] * len(queries),
        [*queries, *pieces, *(states or ())],
        limit=48,
        flops=2 * columns * keys * 512,
        read=keys * 160,
        trans=columns * keys,
    )


def combine_body(head_dim, mine, theirs, out):
    blocks, _, tokens = out.shape
    at = head_dim + 16
    a_top, b_top = mine[at : at + 1], theirs[at : at + 1]
    top = jnp.maximum(a_top, b_top)
    a_part, b_part = jnp.exp2(a_top - top), jnp.exp2(b_top - top)
    total = mine[head_dim : head_dim + 1] * a_part + theirs[head_dim : head_dim + 1] * b_part
    result = (mine[:head_dim] * a_part + theirs[:head_dim] * b_part) / total
    for b in range(blocks):
        out[b] = result[:, b * tokens : (b + 1) * tokens].astype(BF16)


def finish_body(attended, inner, merged, attn_out, proj_out, out):
    rows = turned(attended).astype(BF16)
    after = (inner[...].astype(F32) + dot(rows, attn_out[...])).astype(BF16)
    out[...] = (merged[...].astype(F32) + dot(after, proj_out[...])).T.astype(BF16)


def local(
    features,
    hint,
    conv_weight,
    conv_bias,
    zero_weight,
    zero_bias,
    group_gain,
    proj_in,
    norm_gain,
    query_weight,
    key_weight,
    value_weight,
    attn_out,
    proj_out,
):
    tokens, channels = features.shape
    head_dim = channels // HEADS
    everyone = lax.axis_size(SEQ)
    shape = jax.ShapeDtypeStruct
    hint, features = hint.T, features.T
    core = lax.axis_index("c").reshape(1)
    swap = [(0, 1), (1, 0)]
    ends = [(i, i + 1) for i in range(1, everyone - 1, 2)]
    odd = lax.ppermute(hint, SEQ, ends + [(b, a) for a, b in ends])
    pair = lax.ppermute(hint, "c", swap)
    line = shape((1, channels), F32)
    partial, odd_weight, features, zero_weight, zero_bias, group_gain, norm_gain = call(
        own_row_body,
        [
            shape((tokens, channels), F32),
            shape(conv_weight.shape[1:], BF16),
            shape((tokens, channels), F32),
            shape(zero_weight.shape, BF16),
            line,
            line,
            line,
        ],
        (core, pair, conv_bias, zero_bias, group_gain, norm_gain, hint, conv_weight, features, zero_weight),
        scratch=[
            pltpu.VMEM(hint.shape, BF16),
            pltpu.VMEM((2, *conv_weight.shape[1:]), BF16),
            pltpu.VMEM(features.shape, BF16),
            pltpu.SemaphoreType.DMA((6,)),
        ],
        smem=1,
        away=4,
        limit=53,
        flops=2 * tokens * channels * channels * 6,
        read=10 * channels * channels * 2,
    )
    merged, stats = call(
        merge_body,
        [shape((tokens, channels), BF16), shape((everyone, 128), F32)],
        (partial, odd, odd_weight, zero_weight, zero_bias, features),
        flops=2 * tokens * channels * channels * 4,
        read=4 * channels * channels * 2,
    )
    stats = lax.all_to_all(stats, SEQ, 0, 0, tiled=True)
    inner, send = call(
        project_body,
        [shape((tokens, channels), BF16), shape((HEADS, 128, tokens), BF16)],
        (stats, merged, group_gain, proj_in, norm_gain, query_weight, key_weight, value_weight),
        flops=2 * tokens * channels * channels * 4,
        read=4 * channels * channels * 2,
    )
    received = lax.all_to_all(send, "z", 0, 0, tiled=True)
    depth = 128 - 2 * head_dim
    queries, pair = received[:, :depth, :], received[:, depth:, :]
    chips = lax.axis_size("x")
    ring = lambda by: [(i, (i + by) % chips) for i in range(chips)]
    pieces = [lax.ppermute(pair, "x", ring(by)) for by in (chips - 1, 2, 1)]
    others = lax.ppermute(queries, "c", swap)
    states = attend([queries, others], [pair], None, head_dim)
    (theirs,) = attend([others], pieces, states[1:], head_dim)
    back = lax.ppermute(theirs, "c", swap)
    (mine,) = attend([queries], pieces, states[:1], head_dim)
    result = call(
        functools.partial(combine_body, head_dim), shape((HEADS, head_dim, tokens), BF16), (mine, back)
    )
    attended = lax.all_to_all(result, "z", 0, 0, tiled=True).reshape(channels, tokens)
    return call(
        finish_body,
        shape((channels, tokens), BF16),
        (attended, inner, merged, attn_out, proj_out),
        flops=2 * tokens * channels * channels * 2,
        read=2 * channels * channels * 2,
    ).T


def solution(mesh):
    torus = Mesh(mesh.devices.reshape(mesh.shape["dp"], 4, 8, 2), DP_SEQ)
    return jax.shard_map(
        local,
        mesh=torus,
        in_specs=(P(DP_SEQ, None), P(DP_SEQ, None)) + (P(),) * 12,
        out_specs=P(DP_SEQ, None),
        check_vma=False,
    )
```

```python
import functools
import math

import jax
import jax.numpy as jnp
from jax import lax
from jax.experimental import pallas as pl
from jax.experimental.pallas import tpu as pltpu
from jax.sharding import Mesh
from jax.sharding import PartitionSpec as P

HEADS = 8
GROUPS = 32
WIDTH = 128
SEQ = ("x", "z", "c")
DP_SEQ = ("dp", "x", "z", "c")
NORM_EPS = 1e-06
LAYER_EPS = 1e-05
HIGHEST = lax.Precision.HIGHEST
F32 = jnp.float32
BF16 = jnp.bfloat16
VMEM = pl.BlockSpec(memory_space=pltpu.VMEM)
SMEM = pl.BlockSpec(memory_space=pltpu.SMEM)
MIB = 1024 * 1024


def dot(a, b):
    return jnp.dot(a, b, preferred_element_type=F32)


def exact_dot(a, b):
    return jnp.dot(a, b, precision=HIGHEST, preferred_element_type=F32)


def call(body, out_shape, args, scratch=(), limit=24, flops=0, read=0, trans=0, smem=0):
    many = isinstance(out_shape, (list, tuple))
    return pl.pallas_call(
        body,
        out_shape=out_shape,
        in_specs=[SMEM] * smem + [VMEM] * (len(args) - smem),
        out_specs=[VMEM] * len(out_shape) if many else VMEM,
        scratch_shapes=scratch,
        compiler_params=pltpu.CompilerParams(vmem_limit_bytes=limit * MIB),
        cost_estimate=pl.CostEstimate(flops=flops, bytes_accessed=read, transcendentals=trans),
    )(*args)


def group_spread(channels, lanes, first):
    per_group = channels // GROUPS
    lane = lax.broadcasted_iota(jnp.int32, (lanes, channels), 0)
    chan = lax.broadcasted_iota(jnp.int32, (lanes, channels), 1)
    low = (lane - first) * per_group
    inside = (chan >= low) & (chan < low + per_group) & (lane >= first) & (lane < first + GROUPS)
    return inside.astype(F32)


def group_gather(channels, lanes, first):
    per_group = channels // GROUPS
    lane = lax.broadcasted_iota(jnp.int32, (channels, lanes), 1)
    chan = lax.broadcasted_iota(jnp.int32, (channels, lanes), 0)
    low = (lane - first) * per_group
    inside = (chan >= low) & (chan < low + per_group) & (lane >= first) & (lane < first + GROUPS)
    return inside.astype(F32)


def turned(ref):
    return ref[...].astype(F32).T


def masks_body(_, gather_low, gather_high, spread_low, spread_high):
    channels, lanes = gather_low.shape
    gather_low[...] = group_gather(channels, lanes, 0)
    gather_high[...] = group_gather(channels, lanes, GROUPS)
    spread_low[...] = group_spread(channels, lanes, 0)
    spread_high[...] = group_spread(channels, lanes, GROUPS)


def taps(wide, weight, index):
    tokens, channels = wide.shape
    column = lax.broadcasted_iota(jnp.int32, (tokens, channels), 0)
    left = jnp.where(column == 0, 0.0, pltpu.roll(wide, 1, 0)).astype(BF16)
    right = jnp.where(column == tokens - 1, 0.0, pltpu.roll(wide, tokens - 1, 0)).astype(BF16)
    at = (lambda b: b) if index is None else (lambda b: (index, b))
    total = dot(left, weight[at(0)])
    total += dot(wide.astype(BF16), weight[at(1)])
    return total + dot(right, weight[at(2)])


def own_row_body(core, hint, pair, weight, bias, features, mask, partial, odd_weight, features_out):
    pair_row = 2 - 2 * core[0]
    partial[...] = (
        taps(turned(hint), weight, 1)
        + taps(turned(pair), weight, pair_row)
        + bias[...].reshape(1, partial.shape[1])
    )
    odd_weight[...] = weight[2 - pair_row]
    features_out[...] = turned(features)


def merge_body(
    partial, odd, odd_weight, zero_weight, zero_bias, features, gather_low, gather_high, spread_low, merged_out, stats_out
):
    conv = partial[...] + taps(turned(odd), odd_weight, None)
    control = (conv / (1.0 + jnp.exp(-conv))).astype(BF16)
    branch = dot(control, zero_weight[...]) + zero_bias[...].reshape(1, partial.shape[1])
    merged = (features[...] + branch).astype(BF16)
    merged_out[...] = merged
    wide = merged.astype(F32)
    tokens, channels = wide.shape
    entries = tokens * (channels // GROUPS)
    mean = exact_dot(jnp.sum(wide, axis=0, keepdims=True), gather_low[...]) / entries
    centred = wide - exact_dot(mean, spread_low[...])
    square = exact_dot(jnp.sum(centred * centred, axis=0, keepdims=True), gather_high[...])
    stats_out[...] = jnp.broadcast_to(mean + square / entries, stats_out.shape)


def project_body(
    stats, merged, group_gain, proj_in, norm_gain, wq, wk, wv, spread_low, spread_high, inner_out, send
):
    channels = merged.shape[1]
    head_dim = channels // HEADS
    everyone = stats[...]
    average = jnp.mean(everyone, axis=0, keepdims=True)
    between = jnp.mean(jnp.square(everyone - average), axis=0, keepdims=True)
    mean = exact_dot(average, spread_low[...])
    variance = exact_dot(average, spread_high[...]) + exact_dot(between, spread_low[...])
    factor = lax.rsqrt(variance + NORM_EPS)
    grouped = ((merged[...].astype(F32) - mean) * factor * group_gain[...].reshape(1, channels)).astype(BF16)
    inner = dot(grouped, proj_in[...]).astype(BF16)
    inner_out[...] = inner
    wide = inner.astype(F32)
    centred = wide - jnp.mean(wide, axis=1, keepdims=True)
    variance = jnp.mean(centred * centred, axis=1, keepdims=True)
    normed = (centred * lax.rsqrt(variance + LAYER_EPS) * norm_gain[...].reshape(1, channels)).astype(BF16)
    scale = math.log2(math.e) / math.sqrt(head_dim)
    queries = (dot(normed, wq[...]) * scale).T
    keys = dot(normed, wk[...]).T
    values = dot(normed, wv[...]).T
    for h in range(HEADS):
        rows = slice(h * head_dim, (h + 1) * head_dim)
        block = jnp.concatenate([queries[rows], keys[rows], values[rows]], axis=0)
        send[h] = block.astype(BF16)


def attend_body(head_dim, first, n_queries, n_pieces, *refs):
    query_refs, refs = refs[:n_queries], refs[n_queries:]
    pieces, refs = refs[:n_pieces], refs[n_pieces:]
    if not first:
        states, refs = refs[:n_queries], refs[n_queries:]
    depth = head_dim + 8
    side_by_side = lambda ref: jnp.concatenate([ref[b] for b in range(ref.shape[0])], axis=1)
    pairs = [side_by_side(piece) for piece in pieces]
    keys = [pair[:depth].astype(F32).T.astype(BF16) for pair in pairs]
    ones = jnp.ones((16, pairs[0].shape[1]), BF16)
    summed = jnp.concatenate([jnp.concatenate([pair, ones], axis=0) for pair in pairs], axis=1)
    rows = summed.shape[0] - head_dim
    for n, query_ref in enumerate(query_refs):
        queries = side_by_side(query_ref)
        queries = jnp.concatenate([queries, jnp.zeros((8, queries.shape[1]), BF16)], axis=0)
        scores = [dot(k, queries) for k in keys]
        top = functools.reduce(jnp.maximum, [jnp.max(s, axis=0, keepdims=True) for s in scores])
        if not first:
            before = states[n][rows : rows + 1, :]
            top = jnp.maximum(top, before)
        probs = jnp.concatenate([jnp.exp2(s - top).astype(BF16) for s in scores], axis=0)
        total = dot(summed, probs)[head_dim:]
        if not first:
            total += states[n][:rows, :] * jnp.exp2(before - top)
        refs[n][:rows, :] = total
        refs[n][rows:, :] = jnp.broadcast_to(top, (8, top.shape[1]))


def attend(queries, pieces, states, head_dim):
    blocks, _, tokens = queries[0].shape
    columns = blocks * tokens
    keys = sum(p.shape[0] * p.shape[2] for p in pieces) * len(queries)
    return call(
        functools.partial(attend_body, head_dim, states is None, len(queries), len(pieces)),
        [jax.ShapeDtypeStruct((head_dim + 24, columns), F32)] * len(queries),
        [*queries, *pieces, *(states or ())],
        limit=48,
        flops=2 * columns * keys * 512,
        read=keys * 160,
        trans=columns * keys,
    )


def combine_body(head_dim, mine, theirs, out):
    blocks, _, tokens = out.shape
    at = head_dim + 16
    a_top, b_top = mine[at : at + 1], theirs[at : at + 1]
    top = jnp.maximum(a_top, b_top)
    a_part, b_part = jnp.exp2(a_top - top), jnp.exp2(b_top - top)
    total = mine[head_dim : head_dim + 1] * a_part + theirs[head_dim : head_dim + 1] * b_part
    result = (mine[:head_dim] * a_part + theirs[:head_dim] * b_part) / total
    for b in range(blocks):
        out[b] = result[:, b * tokens : (b + 1) * tokens].astype(BF16)


def finish_body(attended, inner, merged, attn_out, proj_out, out):
    rows = turned(attended).astype(BF16)
    after = (inner[...].astype(F32) + dot(rows, attn_out[...])).astype(BF16)
    out[...] = (merged[...].astype(F32) + dot(after, proj_out[...])).T.astype(BF16)


def local(
    features,
    hint,
    conv_weight,
    conv_bias,
    zero_weight,
    zero_bias,
    group_gain,
    proj_in,
    norm_gain,
    query_weight,
    key_weight,
    value_weight,
    attn_out,
    proj_out,
):
    tokens, channels = features.shape
    head_dim = channels // HEADS
    everyone = lax.axis_size(SEQ)
    shape = jax.ShapeDtypeStruct
    hint, features = hint.T, features.T
    core = lax.axis_index("c").reshape(1)
    swap = [(0, 1), (1, 0)]
    ends = [(i, i + 1) for i in range(1, everyone - 1, 2)]
    odd = lax.ppermute(hint, SEQ, ends + [(b, a) for a, b in ends])
    pair = lax.ppermute(hint, "c", swap)
    masks = call(
        masks_body, [shape((channels, 128), F32)] * 2 + [shape((128, channels), F32)] * 2, (pair,), flops=2000000000
    )
    partial, odd_weight, features = call(
        own_row_body,
        [shape((tokens, channels), F32), shape(conv_weight.shape[1:], BF16), shape((tokens, channels), F32)],
        (core, hint, pair, conv_weight, conv_bias, features, masks[0]),
        smem=1,
        flops=2 * tokens * channels * channels * 6,
        read=10 * channels * channels * 2,
    )
    merged, stats = call(
        merge_body,
        [shape((tokens, channels), BF16), shape((everyone, 128), F32)],
        (partial, odd, odd_weight, zero_weight, zero_bias, features, *masks[:3]),
        flops=2 * tokens * channels * channels * 4,
        read=4 * channels * channels * 2,
    )
    stats = lax.all_to_all(stats, SEQ, 0, 0, tiled=True)
    inner, send = call(
        project_body,
        [shape((tokens, channels), BF16), shape((HEADS, 3 * head_dim, tokens), BF16)],
        (stats, merged, group_gain, proj_in, norm_gain, query_weight, key_weight, value_weight, *masks[2:]),
        flops=2 * tokens * channels * channels * 4,
        read=4 * channels * channels * 2,
    )
    received = lax.all_to_all(send, "z", 0, 0, tiled=True)
    queries, pair = received[:, :head_dim, :], received[:, head_dim:, :]
    chips = lax.axis_size("x")
    ring = lambda by: [(i, (i + by) % chips) for i in range(chips)]
    pieces = [lax.ppermute(pair, "x", ring(by)) for by in (chips - 1, 2, 1)]
    others = lax.ppermute(queries, "c", swap)
    state = attend([queries], [pair], None, head_dim)
    (theirs,) = attend([others], [pair, *pieces], None, head_dim)
    back = lax.ppermute(theirs, "c", swap)
    (mine,) = attend([queries], pieces, state, head_dim)
    result = call(
        functools.partial(combine_body, head_dim), shape((HEADS, head_dim, tokens), BF16), (mine, back)
    )
    attended = lax.all_to_all(result, "z", 0, 0, tiled=True).reshape(channels, tokens)
    return call(
        finish_body,
        shape((channels, tokens), BF16),
        (attended, inner, merged, attn_out, proj_out),
        flops=2 * tokens * channels * channels * 2,
        read=2 * channels * channels * 2,
    ).T


def solution(mesh):
    torus = Mesh(mesh.devices.reshape(mesh.shape["dp"], 4, 8, 2), DP_SEQ)
    return jax.shard_map(
        local,
        mesh=torus,
        in_specs=(P(DP_SEQ, None), P(DP_SEQ, None)) + (P(),) * 12,
        out_specs=P(DP_SEQ, None),
        check_vma=False,
    )
```

```python
import functools
import math

import jax
import jax.numpy as jnp
from jax import lax
from jax.experimental import pallas as pl
from jax.experimental.pallas import tpu as pltpu
from jax.sharding import Mesh
from jax.sharding import PartitionSpec as P

HEADS = 8
GROUPS = 32
WIDTH = 128
SEQ = ("x", "z", "c")
DP_SEQ = ("dp", "x", "z", "c")
NORM_EPS = 1e-06
LAYER_EPS = 1e-05
BOUND_LIMIT = 56.0
HIGHEST = lax.Precision.HIGHEST
F32 = jnp.float32
BF16 = jnp.bfloat16
VMEM = pl.BlockSpec(memory_space=pltpu.VMEM)
SMEM = pl.BlockSpec(memory_space=pltpu.SMEM)
MIB = 1024 * 1024


def dot(a, b):
    return jnp.dot(a, b, preferred_element_type=F32)


def exact_dot(a, b):
    return jnp.dot(a, b, precision=HIGHEST, preferred_element_type=F32)


def call(body, out_shape, args, scratch=(), limit=24, flops=0, read=0, trans=0, smem=0):
    many = isinstance(out_shape, (list, tuple))
    return pl.pallas_call(
        body,
        out_shape=out_shape,
        in_specs=[SMEM] * smem + [VMEM] * (len(args) - smem),
        out_specs=[VMEM] * len(out_shape) if many else VMEM,
        scratch_shapes=scratch,
        compiler_params=pltpu.CompilerParams(vmem_limit_bytes=limit * MIB),
        cost_estimate=pl.CostEstimate(flops=flops, bytes_accessed=read, transcendentals=trans),
    )(*args)


def group_spread(channels, lanes, first):
    per_group = channels // GROUPS
    lane = lax.broadcasted_iota(jnp.int32, (lanes, channels), 0)
    chan = lax.broadcasted_iota(jnp.int32, (lanes, channels), 1)
    low = (lane - first) * per_group
    inside = (chan >= low) & (chan < low + per_group) & (lane >= first) & (lane < first + GROUPS)
    return inside.astype(F32)


def group_gather(channels, lanes, first):
    per_group = channels // GROUPS
    lane = lax.broadcasted_iota(jnp.int32, (channels, lanes), 1)
    chan = lax.broadcasted_iota(jnp.int32, (channels, lanes), 0)
    low = (lane - first) * per_group
    inside = (chan >= low) & (chan < low + per_group) & (lane >= first) & (lane < first + GROUPS)
    return inside.astype(F32)


def turned(ref):
    return ref[...].astype(F32).T


def masks_body(gather_low, gather_high, spread_low, spread_high):
    channels, lanes = gather_low.shape
    gather_low[...] = group_gather(channels, lanes, 0)
    gather_high[...] = group_gather(channels, lanes, GROUPS)
    spread_low[...] = group_spread(channels, lanes, 0)
    spread_high[...] = group_spread(channels, lanes, GROUPS)


def taps(wide, weight, index):
    tokens, channels = wide.shape
    column = lax.broadcasted_iota(jnp.int32, (tokens, channels), 0)
    left = jnp.where(column == 0, 0.0, pltpu.roll(wide, 1, 0)).astype(BF16)
    right = jnp.where(column == tokens - 1, 0.0, pltpu.roll(wide, tokens - 1, 0)).astype(BF16)
    at = (lambda b: b) if index is None else (lambda b: (index, b))
    total = dot(left, weight[at(0)])
    total += dot(wide.astype(BF16), weight[at(1)])
    return total + dot(right, weight[at(2)])


def own_row_body(core, hint, pair, weight, bias, features, mask, partial, odd_weight, features_out):
    pair_row = 2 - 2 * core[0]
    partial[...] = (
        taps(turned(hint), weight, 1)
        + taps(turned(pair), weight, pair_row)
        + bias[...].reshape(1, partial.shape[1])
    )
    odd_weight[...] = weight[2 - pair_row]
    features_out[...] = turned(features)


def merge_body(
    partial, odd, odd_weight, zero_weight, zero_bias, features, gather_low, gather_high, spread_low, merged_out, stats_out
):
    conv = partial[...] + taps(turned(odd), odd_weight, None)
    control = (conv / (1.0 + jnp.exp(-conv))).astype(BF16)
    branch = dot(control, zero_weight[...]) + zero_bias[...].reshape(1, partial.shape[1])
    merged = (features[...] + branch).astype(BF16)
    merged_out[...] = merged
    wide = merged.astype(F32)
    tokens, channels = wide.shape
    entries = tokens * (channels // GROUPS)
    mean = exact_dot(jnp.sum(wide, axis=0, keepdims=True), gather_low[...]) / entries
    centred = wide - exact_dot(mean, spread_low[...])
    square = exact_dot(jnp.sum(centred * centred, axis=0, keepdims=True), gather_high[...])
    stats_out[...] = jnp.broadcast_to(mean + square / entries, stats_out.shape)


def project_body(
    stats, merged, group_gain, proj_in, norm_gain, wq, wk, wv, spread_low, spread_high, inner_out, send
):
    channels = merged.shape[1]
    head_dim = channels // HEADS
    everyone = stats[...]
    average = jnp.mean(everyone, axis=0, keepdims=True)
    between = jnp.mean(jnp.square(everyone - average), axis=0, keepdims=True)
    mean = exact_dot(average, spread_low[...])
    variance = exact_dot(average, spread_high[...]) + exact_dot(between, spread_low[...])
    factor = lax.rsqrt(variance + NORM_EPS)
    grouped = ((merged[...].astype(F32) - mean) * factor * group_gain[...].reshape(1, channels)).astype(BF16)
    inner = dot(grouped, proj_in[...]).astype(BF16)
    inner_out[...] = inner
    wide = inner.astype(F32)
    centred = wide - jnp.mean(wide, axis=1, keepdims=True)
    variance = jnp.mean(centred * centred, axis=1, keepdims=True)
    normed = (centred * lax.rsqrt(variance + LAYER_EPS) * norm_gain[...].reshape(1, channels)).astype(BF16)
    scale = math.log2(math.e) / math.sqrt(head_dim)
    queries = (dot(normed, wq[...]) * scale).T
    keys = dot(normed, wk[...]).T
    values = dot(normed, wv[...]).T
    for h in range(HEADS):
        rows = slice(h * head_dim, (h + 1) * head_dim)
        block = jnp.concatenate([queries[rows], keys[rows], values[rows]], axis=0)
        send[h] = block.astype(BF16)


def squared(vectors):
    wide = vectors.astype(F32)
    return jnp.sum(wide * wide, axis=0, keepdims=True)


def attend_body(head_dim, first, n_queries, n_pieces, *refs):
    query_refs, refs = refs[:n_queries], refs[n_queries:]
    pieces, refs = refs[:n_pieces], refs[n_pieces:]
    if not first:
        states, refs = refs[:n_queries], refs[n_queries:]
    depth = head_dim + 8
    side_by_side = lambda ref: jnp.concatenate([ref[b] for b in range(ref.shape[0])], axis=1)
    pairs = [side_by_side(piece) for piece in pieces]
    keys = [pair[:depth].astype(F32).T.astype(BF16) for pair in pairs]
    ones = jnp.ones((16, pairs[0].shape[1]), BF16)
    summed = jnp.concatenate([jnp.concatenate([pair, ones], axis=0) for pair in pairs], axis=1)
    rows = summed.shape[0] - head_dim
    squares = functools.reduce(jnp.maximum, [squared(pair[:head_dim]) for pair in pairs])
    longest = jnp.sqrt(jnp.max(squares, axis=1, keepdims=True)) * (1.0 + 2.0**-10)
    for n, query_ref in enumerate(query_refs):
        queries = side_by_side(query_ref)
        bound = jnp.sqrt(squared(queries)) * longest
        queries = jnp.concatenate([queries, jnp.zeros((8, queries.shape[1]), BF16)], axis=0)

        def store(top, probs):
            if not first:
                before = states[n][rows : rows + 1, :]
                new_top = jnp.maximum(top, before)
            else:
                new_top = top
            total = dot(summed, jnp.concatenate(probs, axis=0))[head_dim:]
            if not first:
                total = total * jnp.exp2(top - new_top) + states[n][:rows, :] * jnp.exp2(before - new_top)
            refs[n][:rows, :] = total
            refs[n][rows:, :] = jnp.broadcast_to(new_top, (8, new_top.shape[1]))

        safe = jnp.max(bound) <= BOUND_LIMIT

        @pl.when(safe)
        def _():
            store(bound, [jnp.exp2(dot(k, queries) - bound).astype(BF16) for k in keys])

        @pl.when(jnp.logical_not(safe))
        def _():
            scores = [dot(k, queries) for k in keys]
            top = functools.reduce(jnp.maximum, [jnp.max(s, axis=0, keepdims=True) for s in scores])
            store(top, [jnp.exp2(s - top).astype(BF16) for s in scores])


def attend(queries, pieces, states, head_dim):
    blocks, _, tokens = queries[0].shape
    columns = blocks * tokens
    keys = sum(p.shape[0] * p.shape[2] for p in pieces) * len(queries)
    return call(
        functools.partial(attend_body, head_dim, states is None, len(queries), len(pieces)),
        [jax.ShapeDtypeStruct((head_dim + 24, columns), F32)] * len(queries),
        [*queries, *pieces, *(states or ())],
        limit=48,
        flops=2 * columns * keys * 512,
        read=keys * 160,
        trans=columns * keys,
    )


def combine_body(head_dim, mine, theirs, out):
    blocks, _, tokens = out.shape
    at = head_dim + 16
    a_top, b_top = mine[at : at + 1], theirs[at : at + 1]
    top = jnp.maximum(a_top, b_top)
    a_part, b_part = jnp.exp2(a_top - top), jnp.exp2(b_top - top)
    total = mine[head_dim : head_dim + 1] * a_part + theirs[head_dim : head_dim + 1] * b_part
    result = (mine[:head_dim] * a_part + theirs[:head_dim] * b_part) / total
    for b in range(blocks):
        out[b] = result[:, b * tokens : (b + 1) * tokens].astype(BF16)


def finish_body(attended, inner, merged, attn_out, proj_out, out):
    rows = turned(attended).astype(BF16)
    after = (inner[...].astype(F32) + dot(rows, attn_out[...])).astype(BF16)
    out[...] = (merged[...].astype(F32) + dot(after, proj_out[...])).T.astype(BF16)


def local(
    features,
    hint,
    conv_weight,
    conv_bias,
    zero_weight,
    zero_bias,
    group_gain,
    proj_in,
    norm_gain,
    query_weight,
    key_weight,
    value_weight,
    attn_out,
    proj_out,
):
    tokens, channels = features.shape
    head_dim = channels // HEADS
    everyone = lax.axis_size(SEQ)
    shape = jax.ShapeDtypeStruct
    hint, features = hint.T, features.T
    core = lax.axis_index("c").reshape(1)
    swap = [(0, 1), (1, 0)]
    ends = [(i, i + 1) for i in range(1, everyone - 1, 2)]
    odd = lax.ppermute(hint, SEQ, ends + [(b, a) for a, b in ends])
    pair = lax.ppermute(hint, "c", swap)
    masks = call(
        masks_body, [shape((channels, 128), F32)] * 2 + [shape((128, channels), F32)] * 2, (), flops=2000000000
    )
    partial, odd_weight, features = call(
        own_row_body,
        [shape((tokens, channels), F32), shape(conv_weight.shape[1:], BF16), shape((tokens, channels), F32)],
        (core, hint, pair, conv_weight, conv_bias, features, masks[0]),
        smem=1,
        flops=2 * tokens * channels * channels * 6,
        read=10 * channels * channels * 2,
    )
    merged, stats = call(
        merge_body,
        [shape((tokens, channels), BF16), shape((everyone, 128), F32)],
        (partial, odd, odd_weight, zero_weight, zero_bias, features, *masks[:3]),
        flops=2 * tokens * channels * channels * 4,
        read=4 * channels * channels * 2,
    )
    stats = lax.all_to_all(stats, SEQ, 0, 0, tiled=True)
    inner, send = call(
        project_body,
        [shape((tokens, channels), BF16), shape((HEADS, 3 * head_dim, tokens), BF16)],
        (stats, merged, group_gain, proj_in, norm_gain, query_weight, key_weight, value_weight, *masks[2:]),
        flops=2 * tokens * channels * channels * 4,
        read=4 * channels * channels * 2,
    )
    received = lax.all_to_all(send, "z", 0, 0, tiled=True)
    queries, pair = received[:, :head_dim, :], received[:, head_dim:, :]
    chips = lax.axis_size("x")
    ring = lambda by: [(i, (i + by) % chips) for i in range(chips)]
    pieces = [lax.ppermute(pair, "x", ring(by)) for by in (chips - 1, 2, 1)]
    others = lax.ppermute(queries, "c", swap)
    state = attend([queries], [pair], None, head_dim)
    (theirs,) = attend([others], [pair, *pieces], None, head_dim)
    back = lax.ppermute(theirs, "c", swap)
    (mine,) = attend([queries], pieces, state, head_dim)
    result = call(
        functools.partial(combine_body, head_dim), shape((HEADS, head_dim, tokens), BF16), (mine, back)
    )
    attended = lax.all_to_all(result, "z", 0, 0, tiled=True).reshape(channels, tokens)
    return call(
        finish_body,
        shape((channels, tokens), BF16),
        (attended, inner, merged, attn_out, proj_out),
        flops=2 * tokens * channels * channels * 2,
        read=2 * channels * channels * 2,
    ).T


def solution(mesh):
    torus = Mesh(mesh.devices.reshape(mesh.shape["dp"], 4, 8, 2), DP_SEQ)
    return jax.shard_map(
        local,
        mesh=torus,
        in_specs=(P(DP_SEQ, None), P(DP_SEQ, None)) + (P(),) * 12,
        out_specs=P(DP_SEQ, None),
        check_vma=False,
    )
```

```python
import functools
import math

import jax
import jax.numpy as jnp
from jax import lax
from jax.experimental import pallas as pl
from jax.experimental.pallas import tpu as pltpu
from jax.sharding import Mesh
from jax.sharding import PartitionSpec as P

HEADS = 8
GROUPS = 32
WIDTH = 128
SEQ = ("x", "z", "c")
DP_SEQ = ("dp", "x", "z", "c")
NORM_EPS = 1e-06
LAYER_EPS = 1e-05
BOUND_LIMIT = 56.0
F32 = jnp.float32
BF16 = jnp.bfloat16
VMEM = pl.BlockSpec(memory_space=pltpu.VMEM)
SMEM = pl.BlockSpec(memory_space=pltpu.SMEM)
MIB = 1024 * 1024


def dot(a, b):
    return jnp.dot(a, b, preferred_element_type=F32)


def masked_sums(row, mask):
    high = row.astype(BF16).astype(F32)
    middle = (row - high).astype(BF16).astype(F32)
    low = row - high - middle
    parts = jnp.concatenate([high, middle, low, jnp.zeros((5, row.shape[1]), F32)], axis=0).astype(BF16)
    return jnp.sum(dot(parts, mask), axis=0, keepdims=True)


def call(body, out_shape, args, scratch=(), limit=24, flops=0, read=0, trans=0, smem=0):
    many = isinstance(out_shape, (list, tuple))
    return pl.pallas_call(
        body,
        out_shape=out_shape,
        in_specs=[SMEM] * smem + [VMEM] * (len(args) - smem),
        out_specs=[VMEM] * len(out_shape) if many else VMEM,
        scratch_shapes=scratch,
        compiler_params=pltpu.CompilerParams(vmem_limit_bytes=limit * MIB),
        cost_estimate=pl.CostEstimate(flops=flops, bytes_accessed=read, transcendentals=trans),
    )(*args)


def group_spread(channels, lanes, first):
    per_group = channels // GROUPS
    lane = lax.broadcasted_iota(jnp.int32, (lanes, channels), 0)
    chan = lax.broadcasted_iota(jnp.int32, (lanes, channels), 1)
    low = (lane - first) * per_group
    inside = (chan >= low) & (chan < low + per_group) & (lane >= first) & (lane < first + GROUPS)
    return inside.astype(F32).astype(BF16)


def group_gather(channels, lanes, first):
    per_group = channels // GROUPS
    lane = lax.broadcasted_iota(jnp.int32, (channels, lanes), 1)
    chan = lax.broadcasted_iota(jnp.int32, (channels, lanes), 0)
    low = (lane - first) * per_group
    inside = (chan >= low) & (chan < low + per_group) & (lane >= first) & (lane < first + GROUPS)
    return inside.astype(F32).astype(BF16)


def turned(ref):
    return ref[...].astype(F32).T


def masks_body(gather_low, gather_high, spread_low, spread_high):
    channels, lanes = gather_low.shape
    gather_low[...] = group_gather(channels, lanes, 0)
    gather_high[...] = group_gather(channels, lanes, GROUPS)
    spread_low[...] = group_spread(channels, lanes, 0)
    spread_high[...] = group_spread(channels, lanes, GROUPS)


def taps(wide, weight, index):
    tokens, channels = wide.shape
    column = lax.broadcasted_iota(jnp.int32, (tokens, channels), 0)
    left = jnp.where(column == 0, 0.0, pltpu.roll(wide, 1, 0)).astype(BF16)
    right = jnp.where(column == tokens - 1, 0.0, pltpu.roll(wide, tokens - 1, 0)).astype(BF16)
    at = (lambda b: b) if index is None else (lambda b: (index, b))
    total = dot(left, weight[at(0)])
    total += dot(wide.astype(BF16), weight[at(1)])
    return total + dot(right, weight[at(2)])


def own_row_body(core, hint, pair, weight, bias, features, mask, partial, odd_weight, features_out):
    pair_row = 2 - 2 * core[0]
    partial[...] = (
        taps(turned(hint), weight, 1)
        + taps(turned(pair), weight, pair_row)
        + bias[...].reshape(1, partial.shape[1])
    )
    odd_weight[...] = weight[2 - pair_row]
    features_out[...] = turned(features)


def merge_body(
    partial, odd, odd_weight, zero_weight, zero_bias, features, gather_low, gather_high, spread_low, merged_out, stats_out
):
    conv = partial[...] + taps(turned(odd), odd_weight, None)
    control = (conv / (1.0 + jnp.exp(-conv))).astype(BF16)
    branch = dot(control, zero_weight[...]) + zero_bias[...].reshape(1, partial.shape[1])
    merged = (features[...] + branch).astype(BF16)
    merged_out[...] = merged
    wide = merged.astype(F32)
    tokens, channels = wide.shape
    entries = tokens * (channels // GROUPS)
    mean = masked_sums(jnp.sum(wide, axis=0, keepdims=True), gather_low[...]) / entries
    centred = wide - masked_sums(mean, spread_low[...])
    square = masked_sums(jnp.sum(centred * centred, axis=0, keepdims=True), gather_high[...])
    stats_out[...] = jnp.broadcast_to(mean + square / entries, stats_out.shape)


def project_body(
    stats, merged, group_gain, proj_in, norm_gain, wq, wk, wv, spread_low, spread_high, inner_out, send
):
    channels = merged.shape[1]
    head_dim = channels // HEADS
    everyone = stats[...]
    average = jnp.mean(everyone, axis=0, keepdims=True)
    between = jnp.mean(jnp.square(everyone - average), axis=0, keepdims=True)
    mean = masked_sums(average, spread_low[...])
    variance = masked_sums(average, spread_high[...]) + masked_sums(between, spread_low[...])
    factor = lax.rsqrt(variance + NORM_EPS)
    grouped = ((merged[...].astype(F32) - mean) * factor * group_gain[...].reshape(1, channels)).astype(BF16)
    inner = dot(grouped, proj_in[...]).astype(BF16)
    inner_out[...] = inner
    wide = inner.astype(F32)
    centred = wide - jnp.mean(wide, axis=1, keepdims=True)
    variance = jnp.mean(centred * centred, axis=1, keepdims=True)
    normed = (centred * lax.rsqrt(variance + LAYER_EPS) * norm_gain[...].reshape(1, channels)).astype(BF16)
    scale = math.log2(math.e) / math.sqrt(head_dim)
    queries = (dot(normed, wq[...]) * scale).T
    keys = dot(normed, wk[...]).T
    values = dot(normed, wv[...]).T
    for h in range(HEADS):
        rows = slice(h * head_dim, (h + 1) * head_dim)
        block = jnp.concatenate([queries[rows], keys[rows], values[rows]], axis=0)
        send[h] = block.astype(BF16)


def squared(vectors):
    wide = vectors.astype(F32)
    return jnp.sum(wide * wide, axis=0, keepdims=True)


def attend_body(head_dim, first, n_queries, n_pieces, *refs):
    query_refs, refs = refs[:n_queries], refs[n_queries:]
    pieces, refs = refs[:n_pieces], refs[n_pieces:]
    if not first:
        states, refs = refs[:n_queries], refs[n_queries:]
    depth = head_dim + 8
    side_by_side = lambda ref: jnp.concatenate([ref[b] for b in range(ref.shape[0])], axis=1)
    pairs = [side_by_side(piece) for piece in pieces]
    keys = [pair[:depth].astype(F32).T.astype(BF16) for pair in pairs]
    ones = jnp.ones((16, pairs[0].shape[1]), BF16)
    summed = jnp.concatenate([jnp.concatenate([pair, ones], axis=0) for pair in pairs], axis=1)
    rows = summed.shape[0] - head_dim
    squares = functools.reduce(jnp.maximum, [squared(pair[:head_dim]) for pair in pairs])
    longest = jnp.sqrt(jnp.max(squares, axis=1, keepdims=True)) * (1.0 + 2.0**-10)
    for n, query_ref in enumerate(query_refs):
        queries = side_by_side(query_ref)
        bound = jnp.sqrt(squared(queries)) * longest
        queries = jnp.concatenate([queries, jnp.zeros((8, queries.shape[1]), BF16)], axis=0)

        def store(top, probs):
            if not first:
                before = states[n][rows : rows + 1, :]
                new_top = jnp.maximum(top, before)
            else:
                new_top = top
            total = dot(summed, jnp.concatenate(probs, axis=0))[head_dim:]
            if not first:
                total = total * jnp.exp2(top - new_top) + states[n][:rows, :] * jnp.exp2(before - new_top)
            refs[n][:rows, :] = total
            refs[n][rows:, :] = jnp.broadcast_to(new_top, (8, new_top.shape[1]))

        safe = jnp.max(bound) <= BOUND_LIMIT

        @pl.when(safe)
        def _():
            store(bound, [jnp.exp2(dot(k, queries) - bound).astype(BF16) for k in keys])

        @pl.when(jnp.logical_not(safe))
        def _():
            scores = [dot(k, queries) for k in keys]
            top = functools.reduce(jnp.maximum, [jnp.max(s, axis=0, keepdims=True) for s in scores])
            store(top, [jnp.exp2(s - top).astype(BF16) for s in scores])


def attend(queries, pieces, states, head_dim):
    blocks, _, tokens = queries[0].shape
    columns = blocks * tokens
    keys = sum(p.shape[0] * p.shape[2] for p in pieces) * len(queries)
    return call(
        functools.partial(attend_body, head_dim, states is None, len(queries), len(pieces)),
        [jax.ShapeDtypeStruct((head_dim + 24, columns), F32)] * len(queries),
        [*queries, *pieces, *(states or ())],
        limit=48,
        flops=2 * columns * keys * 512,
        read=keys * 160,
        trans=columns * keys,
    )


def combine_body(head_dim, mine, theirs, out):
    blocks, _, tokens = out.shape
    at = head_dim + 16
    a_top, b_top = mine[at : at + 1], theirs[at : at + 1]
    top = jnp.maximum(a_top, b_top)
    a_part, b_part = jnp.exp2(a_top - top), jnp.exp2(b_top - top)
    total = mine[head_dim : head_dim + 1] * a_part + theirs[head_dim : head_dim + 1] * b_part
    result = (mine[:head_dim] * a_part + theirs[:head_dim] * b_part) / total
    for b in range(blocks):
        out[b] = result[:, b * tokens : (b + 1) * tokens].astype(BF16)


def finish_body(attended, inner, merged, attn_out, proj_out, out):
    rows = turned(attended).astype(BF16)
    after = (inner[...].astype(F32) + dot(rows, attn_out[...])).astype(BF16)
    out[...] = (merged[...].astype(F32) + dot(after, proj_out[...])).T.astype(BF16)


def local(
    features,
    hint,
    conv_weight,
    conv_bias,
    zero_weight,
    zero_bias,
    group_gain,
    proj_in,
    norm_gain,
    query_weight,
    key_weight,
    value_weight,
    attn_out,
    proj_out,
):
    tokens, channels = features.shape
    head_dim = channels // HEADS
    everyone = lax.axis_size(SEQ)
    shape = jax.ShapeDtypeStruct
    hint, features = hint.T, features.T
    core = lax.axis_index("c").reshape(1)
    swap = [(0, 1), (1, 0)]
    ends = [(i, i + 1) for i in range(1, everyone - 1, 2)]
    odd = lax.ppermute(hint, SEQ, ends + [(b, a) for a, b in ends])
    pair = lax.ppermute(hint, "c", swap)
    masks = call(
        masks_body, [shape((channels, 128), BF16)] * 2 + [shape((128, channels), BF16)] * 2, (), flops=2000000000
    )
    partial, odd_weight, features = call(
        own_row_body,
        [shape((tokens, channels), F32), shape(conv_weight.shape[1:], BF16), shape((tokens, channels), F32)],
        (core, hint, pair, conv_weight, conv_bias, features, masks[0]),
        smem=1,
        flops=2 * tokens * channels * channels * 6,
        read=10 * channels * channels * 2,
    )
    merged, stats = call(
        merge_body,
        [shape((tokens, channels), BF16), shape((everyone, 128), F32)],
        (partial, odd, odd_weight, zero_weight, zero_bias, features, *masks[:3]),
        flops=2 * tokens * channels * channels * 4,
        read=4 * channels * channels * 2,
    )
    stats = lax.all_to_all(stats, SEQ, 0, 0, tiled=True)
    inner, send = call(
        project_body,
        [shape((tokens, channels), BF16), shape((HEADS, 3 * head_dim, tokens), BF16)],
        (stats, merged, group_gain, proj_in, norm_gain, query_weight, key_weight, value_weight, *masks[2:]),
        flops=2 * tokens * channels * channels * 4,
        read=4 * channels * channels * 2,
    )
    received = lax.all_to_all(send, "z", 0, 0, tiled=True)
    queries, pair = received[:, :head_dim, :], received[:, head_dim:, :]
    chips = lax.axis_size("x")
    ring = lambda by: [(i, (i + by) % chips) for i in range(chips)]
    pieces = [lax.ppermute(pair, "x", ring(by)) for by in (chips - 1, 2, 1)]
    others = lax.ppermute(queries, "c", swap)
    state = attend([queries], [pair], None, head_dim)
    other_state = attend([others], [pair], None, head_dim)
    (theirs,) = attend([others], pieces, other_state, head_dim)
    back = lax.ppermute(theirs, "c", swap)
    (mine,) = attend([queries], pieces, state, head_dim)
    result = call(
        functools.partial(combine_body, head_dim), shape((HEADS, head_dim, tokens), BF16), (mine, back)
    )
    attended = lax.all_to_all(result, "z", 0, 0, tiled=True).reshape(channels, tokens)
    return call(
        finish_body,
        shape((channels, tokens), BF16),
        (attended, inner, merged, attn_out, proj_out),
        flops=2 * tokens * channels * channels * 2,
        read=2 * channels * channels * 2,
    ).T


def solution(mesh):
    torus = Mesh(mesh.devices.reshape(mesh.shape["dp"], 4, 8, 2), DP_SEQ)
    return jax.shard_map(
        local,
        mesh=torus,
        in_specs=(P(DP_SEQ, None), P(DP_SEQ, None)) + (P(),) * 12,
        out_specs=P(DP_SEQ, None),
        check_vma=False,
    )
```

```python
import functools
import math

import jax
import jax.numpy as jnp
from jax import lax
from jax.experimental import pallas as pl
from jax.experimental.pallas import tpu as pltpu
from jax.sharding import Mesh
from jax.sharding import PartitionSpec as P

HEADS = 8
GROUPS = 32
WIDTH = 128
SEQ = ("x", "z", "c")
DP_SEQ = ("dp", "x", "z", "c")
NORM_EPS = 1e-06
LAYER_EPS = 1e-05
BOUND_LIMIT = 56.0
F32 = jnp.float32
BF16 = jnp.bfloat16
VMEM = pl.BlockSpec(memory_space=pltpu.VMEM)
SMEM = pl.BlockSpec(memory_space=pltpu.SMEM)
MIB = 1024 * 1024


def dot(a, b):
    return jnp.dot(a, b, preferred_element_type=F32)


def masked_sums(row, mask):
    high = row.astype(BF16).astype(F32)
    middle = (row - high).astype(BF16).astype(F32)
    low = row - high - middle
    parts = jnp.concatenate([high, middle, low, jnp.zeros((5, row.shape[1]), F32)], axis=0).astype(BF16)
    return jnp.sum(dot(parts, mask), axis=0, keepdims=True)


def call(body, out_shape, args, scratch=(), limit=24, flops=0, read=0, trans=0, smem=0):
    many = isinstance(out_shape, (list, tuple))
    return pl.pallas_call(
        body,
        out_shape=out_shape,
        in_specs=[SMEM] * smem + [VMEM] * (len(args) - smem),
        out_specs=[VMEM] * len(out_shape) if many else VMEM,
        scratch_shapes=scratch,
        compiler_params=pltpu.CompilerParams(vmem_limit_bytes=limit * MIB),
        cost_estimate=pl.CostEstimate(flops=flops, bytes_accessed=read, transcendentals=trans),
    )(*args)


def group_spread(channels, lanes, first):
    per_group = channels // GROUPS
    lane = lax.broadcasted_iota(jnp.int32, (lanes, channels), 0)
    chan = lax.broadcasted_iota(jnp.int32, (lanes, channels), 1)
    low = (lane - first) * per_group
    inside = (chan >= low) & (chan < low + per_group) & (lane >= first) & (lane < first + GROUPS)
    return inside.astype(F32).astype(BF16)


def group_gather(channels, lanes, first):
    per_group = channels // GROUPS
    lane = lax.broadcasted_iota(jnp.int32, (channels, lanes), 1)
    chan = lax.broadcasted_iota(jnp.int32, (channels, lanes), 0)
    low = (lane - first) * per_group
    inside = (chan >= low) & (chan < low + per_group) & (lane >= first) & (lane < first + GROUPS)
    return inside.astype(F32).astype(BF16)


def turned(ref):
    return ref[...].astype(F32).T


def masks_body(gather_low, gather_high, spread_low, spread_high):
    channels, lanes = gather_low.shape
    gather_low[...] = group_gather(channels, lanes, 0)
    gather_high[...] = group_gather(channels, lanes, GROUPS)
    spread_low[...] = group_spread(channels, lanes, 0)
    spread_high[...] = group_spread(channels, lanes, GROUPS)


def taps(wide, weight, index):
    tokens, channels = wide.shape
    column = lax.broadcasted_iota(jnp.int32, (tokens, channels), 0)
    left = jnp.where(column == 0, 0.0, pltpu.roll(wide, 1, 0)).astype(BF16)
    right = jnp.where(column == tokens - 1, 0.0, pltpu.roll(wide, tokens - 1, 0)).astype(BF16)
    at = (lambda b: b) if index is None else (lambda b: (index, b))
    total = dot(left, weight[at(0)])
    total += dot(wide.astype(BF16), weight[at(1)])
    return total + dot(right, weight[at(2)])


def own_row_body(core, hint, pair, weight, bias, features, mask, partial, odd_weight, features_out):
    pair_row = 2 - 2 * core[0]
    partial[...] = (
        taps(turned(hint), weight, 1)
        + taps(turned(pair), weight, pair_row)
        + bias[...].reshape(1, partial.shape[1])
    )
    odd_weight[...] = weight[2 - pair_row]
    features_out[...] = turned(features)


def merge_body(
    partial, odd, odd_weight, zero_weight, zero_bias, features, gather_low, gather_high, spread_low, merged_out, stats_out
):
    conv = partial[...] + taps(turned(odd), odd_weight, None)
    control = (conv / (1.0 + jnp.exp(-conv))).astype(BF16)
    branch = dot(control, zero_weight[...]) + zero_bias[...].reshape(1, partial.shape[1])
    merged = (features[...] + branch).astype(BF16)
    merged_out[...] = merged
    wide = merged.astype(F32)
    tokens, channels = wide.shape
    entries = tokens * (channels // GROUPS)
    mean = masked_sums(jnp.sum(wide, axis=0, keepdims=True), gather_low[...]) / entries
    centred = wide - masked_sums(mean, spread_low[...])
    square = masked_sums(jnp.sum(centred * centred, axis=0, keepdims=True), gather_high[...])
    stats_out[...] = jnp.broadcast_to(mean + square / entries, stats_out.shape)


def project_body(
    stats, merged, group_gain, proj_in, norm_gain, wq, wk, wv, spread_low, spread_high, inner_out, send
):
    channels = merged.shape[1]
    head_dim = channels // HEADS
    everyone = stats[...]
    average = jnp.mean(everyone, axis=0, keepdims=True)
    between = jnp.mean(jnp.square(everyone - average), axis=0, keepdims=True)
    mean = masked_sums(average, spread_low[...])
    variance = masked_sums(average, spread_high[...]) + masked_sums(between, spread_low[...])
    factor = lax.rsqrt(variance + NORM_EPS)
    grouped = ((merged[...].astype(F32) - mean) * factor * group_gain[...].reshape(1, channels)).astype(BF16)
    inner = dot(grouped, proj_in[...]).astype(BF16)
    inner_out[...] = inner
    wide = inner.astype(F32)
    centred = wide - jnp.mean(wide, axis=1, keepdims=True)
    variance = jnp.mean(centred * centred, axis=1, keepdims=True)
    normed = (centred * lax.rsqrt(variance + LAYER_EPS) * norm_gain[...].reshape(1, channels)).astype(BF16)
    scale = math.log2(math.e) / math.sqrt(head_dim)
    queries = (dot(normed, wq[...]) * scale).T
    keys = dot(normed, wk[...]).T
    values = dot(normed, wv[...]).T
    for h in range(HEADS):
        rows = slice(h * head_dim, (h + 1) * head_dim)
        block = jnp.concatenate([queries[rows], keys[rows], values[rows]], axis=0)
        send[h] = block.astype(BF16)


def squared(vectors):
    wide = vectors.astype(F32)
    return jnp.sum(wide * wide, axis=0, keepdims=True)


def attend_body(head_dim, first, n_queries, n_pieces, *refs):
    query_refs, refs = refs[:n_queries], refs[n_queries:]
    pieces, refs = refs[:n_pieces], refs[n_pieces:]
    if not first:
        states, refs = refs[:n_queries], refs[n_queries:]
    depth = head_dim + 8
    side_by_side = lambda ref: jnp.concatenate([ref[b] for b in range(ref.shape[0])], axis=1)
    pairs = [side_by_side(piece) for piece in pieces]
    keys = [pair[:depth].astype(F32).T.astype(BF16) for pair in pairs]
    ones = jnp.ones((16, pairs[0].shape[1]), BF16)
    summed = jnp.concatenate([jnp.concatenate([pair, ones], axis=0) for pair in pairs], axis=1)
    rows = summed.shape[0] - head_dim
    squares = functools.reduce(jnp.maximum, [squared(pair[:head_dim]) for pair in pairs])
    longest = jnp.sqrt(jnp.max(squares, axis=1, keepdims=True)) * (1.0 + 2.0**-10)
    for n, query_ref in enumerate(query_refs):
        queries = side_by_side(query_ref)
        bound = jnp.sqrt(squared(queries)) * longest
        queries = jnp.concatenate([queries, jnp.zeros((8, queries.shape[1]), BF16)], axis=0)

        def store(top, probs):
            if not first:
                before = states[n][rows : rows + 1, :]
                new_top = jnp.maximum(top, before)
            else:
                new_top = top
            total = dot(summed, jnp.concatenate(probs, axis=0))[head_dim:]
            if not first:
                total = total * jnp.exp2(top - new_top) + states[n][:rows, :] * jnp.exp2(before - new_top)
            refs[n][:rows, :] = total
            refs[n][rows:, :] = jnp.broadcast_to(new_top, (8, new_top.shape[1]))

        safe = jnp.max(bound) <= BOUND_LIMIT

        @pl.when(safe)
        def _():
            store(bound, [jnp.exp2(dot(k, queries) - bound).astype(BF16) for k in keys])

        @pl.when(jnp.logical_not(safe))
        def _():
            scores = [dot(k, queries) for k in keys]
            top = functools.reduce(jnp.maximum, [jnp.max(s, axis=0, keepdims=True) for s in scores])
            store(top, [jnp.exp2(s - top).astype(BF16) for s in scores])


def attend(queries, pieces, states, head_dim):
    blocks, _, tokens = queries[0].shape
    columns = blocks * tokens
    keys = sum(p.shape[0] * p.shape[2] for p in pieces) * len(queries)
    return call(
        functools.partial(attend_body, head_dim, states is None, len(queries), len(pieces)),
        [jax.ShapeDtypeStruct((head_dim + 24, columns), F32)] * len(queries),
        [*queries, *pieces, *(states or ())],
        limit=48,
        flops=2 * columns * keys * 512,
        read=keys * 160,
        trans=columns * keys,
    )


def combine_body(head_dim, mine, theirs, out):
    blocks, _, tokens = out.shape
    at = head_dim + 16
    a_top, b_top = mine[at : at + 1], theirs[at : at + 1]
    top = jnp.maximum(a_top, b_top)
    a_part, b_part = jnp.exp2(a_top - top), jnp.exp2(b_top - top)
    total = mine[head_dim : head_dim + 1] * a_part + theirs[head_dim : head_dim + 1] * b_part
    result = (mine[:head_dim] * a_part + theirs[:head_dim] * b_part) / total
    for b in range(blocks):
        out[b] = result[:, b * tokens : (b + 1) * tokens].astype(BF16)


def finish_body(attended, inner, merged, attn_out, proj_out, out):
    rows = turned(attended).astype(BF16)
    after = (inner[...].astype(F32) + dot(rows, attn_out[...])).astype(BF16)
    out[...] = (merged[...].astype(F32) + dot(after, proj_out[...])).T.astype(BF16)


def local(
    features,
    hint,
    conv_weight,
    conv_bias,
    zero_weight,
    zero_bias,
    group_gain,
    proj_in,
    norm_gain,
    query_weight,
    key_weight,
    value_weight,
    attn_out,
    proj_out,
):
    tokens, channels = features.shape
    head_dim = channels // HEADS
    everyone = lax.axis_size(SEQ)
    shape = jax.ShapeDtypeStruct
    hint, features = hint.T, features.T
    core = lax.axis_index("c").reshape(1)
    swap = [(0, 1), (1, 0)]
    ends = [(i, i + 1) for i in range(1, everyone - 1, 2)]
    odd = lax.ppermute(hint, SEQ, ends + [(b, a) for a, b in ends])
    pair = lax.ppermute(hint, "c", swap)
    masks = call(
        masks_body, [shape((channels, 128), BF16)] * 2 + [shape((128, channels), BF16)] * 2, (), flops=1000000000
    )
    partial, odd_weight, features = call(
        own_row_body,
        [shape((tokens, channels), F32), shape(conv_weight.shape[1:], BF16), shape((tokens, channels), F32)],
        (core, hint, pair, conv_weight, conv_bias, features, masks[0]),
        smem=1,
        flops=2 * tokens * channels * channels * 6,
        read=10 * channels * channels * 2,
    )
    merged, stats = call(
        merge_body,
        [shape((tokens, channels), BF16), shape((everyone, 128), F32)],
        (partial, odd, odd_weight, zero_weight, zero_bias, features, *masks[:3]),
        flops=2 * tokens * channels * channels * 4,
        read=4 * channels * channels * 2,
    )
    stats = lax.all_to_all(stats, SEQ, 0, 0, tiled=True)
    inner, send = call(
        project_body,
        [shape((tokens, channels), BF16), shape((HEADS, 3 * head_dim, tokens), BF16)],
        (stats, merged, group_gain, proj_in, norm_gain, query_weight, key_weight, value_weight, *masks[2:]),
        flops=2 * tokens * channels * channels * 4,
        read=4 * channels * channels * 2,
    )
    received = lax.all_to_all(send, "z", 0, 0, tiled=True)
    queries, pair = received[:, :head_dim, :], received[:, head_dim:, :]
    chips = lax.axis_size("x")
    ring = lambda by: [(i, (i + by) % chips) for i in range(chips)]
    pieces = [lax.ppermute(pair, "x", ring(by)) for by in (chips - 1, 2, 1)]
    others = lax.ppermute(queries, "c", swap)
    state = attend([queries], [pair], None, head_dim)
    other_state = attend([others], [pair, pieces[2]], None, head_dim)
    (theirs,) = attend([others], pieces[:2], other_state, head_dim)
    back = lax.ppermute(theirs, "c", swap)
    (mine,) = attend([queries], pieces, state, head_dim)
    result = call(
        functools.partial(combine_body, head_dim), shape((HEADS, head_dim, tokens), BF16), (mine, back)
    )
    attended = lax.all_to_all(result, "z", 0, 0, tiled=True).reshape(channels, tokens)
    return call(
        finish_body,
        shape((channels, tokens), BF16),
        (attended, inner, merged, attn_out, proj_out),
        flops=2 * tokens * channels * channels * 2,
        read=2 * channels * channels * 2,
    ).T


def solution(mesh):
    torus = Mesh(mesh.devices.reshape(mesh.shape["dp"], 4, 8, 2), DP_SEQ)
    return jax.shard_map(
        local,
        mesh=torus,
        in_specs=(P(DP_SEQ, None), P(DP_SEQ, None)) + (P(),) * 12,
        out_specs=P(DP_SEQ, None),
        check_vma=False,
    )
```

```python
import functools
import math

import jax
import jax.numpy as jnp
from jax import lax
from jax.experimental import pallas as pl
from jax.experimental.pallas import tpu as pltpu
from jax.sharding import Mesh
from jax.sharding import PartitionSpec as P

HEADS = 8
GROUPS = 32
WIDTH = 128
SEQ = ("x", "z", "c")
DP_SEQ = ("dp", "x", "z", "c")
NORM_EPS = 1e-06
LAYER_EPS = 1e-05
BOUND_LIMIT = 56.0
F32 = jnp.float32
BF16 = jnp.bfloat16
VMEM = pl.BlockSpec(memory_space=pltpu.VMEM)
SMEM = pl.BlockSpec(memory_space=pltpu.SMEM)
MIB = 1024 * 1024


def dot(a, b):
    return jnp.dot(a, b, preferred_element_type=F32)


def masked_sums(row, mask):
    high = row.astype(BF16).astype(F32)
    middle = (row - high).astype(BF16).astype(F32)
    low = row - high - middle
    parts = jnp.concatenate([high, middle, low, jnp.zeros((5, row.shape[1]), F32)], axis=0).astype(BF16)
    return jnp.sum(dot(parts, mask), axis=0, keepdims=True)


def call(body, out_shape, args, scratch=(), limit=24, flops=0, read=0, trans=0, smem=0):
    many = isinstance(out_shape, (list, tuple))
    return pl.pallas_call(
        body,
        out_shape=out_shape,
        in_specs=[SMEM] * smem + [VMEM] * (len(args) - smem),
        out_specs=[VMEM] * len(out_shape) if many else VMEM,
        scratch_shapes=scratch,
        compiler_params=pltpu.CompilerParams(vmem_limit_bytes=limit * MIB),
        cost_estimate=pl.CostEstimate(flops=flops, bytes_accessed=read, transcendentals=trans),
    )(*args)


def group_spread(channels, lanes, first):
    per_group = channels // GROUPS
    lane = lax.broadcasted_iota(jnp.int32, (lanes, channels), 0)
    chan = lax.broadcasted_iota(jnp.int32, (lanes, channels), 1)
    low = (lane - first) * per_group
    inside = (chan >= low) & (chan < low + per_group) & (lane >= first) & (lane < first + GROUPS)
    return inside.astype(F32).astype(BF16)


def group_gather(channels, lanes, first):
    per_group = channels // GROUPS
    lane = lax.broadcasted_iota(jnp.int32, (channels, lanes), 1)
    chan = lax.broadcasted_iota(jnp.int32, (channels, lanes), 0)
    low = (lane - first) * per_group
    inside = (chan >= low) & (chan < low + per_group) & (lane >= first) & (lane < first + GROUPS)
    return inside.astype(F32).astype(BF16)


def turned(ref):
    return ref[...].astype(F32).T


def masks_body(gather_low, gather_high, spread_low, spread_high):
    channels, lanes = gather_low.shape
    gather_low[...] = group_gather(channels, lanes, 0)
    gather_high[...] = group_gather(channels, lanes, GROUPS)
    spread_low[...] = group_spread(channels, lanes, 0)
    spread_high[...] = group_spread(channels, lanes, GROUPS)


def taps(wide, weight, index):
    tokens, channels = wide.shape
    column = lax.broadcasted_iota(jnp.int32, (tokens, channels), 0)
    left = jnp.where(column == 0, 0.0, pltpu.roll(wide, 1, 0)).astype(BF16)
    right = jnp.where(column == tokens - 1, 0.0, pltpu.roll(wide, tokens - 1, 0)).astype(BF16)
    at = (lambda b: b) if index is None else (lambda b: (index, b))
    total = dot(left, weight[at(0)])
    total += dot(wide.astype(BF16), weight[at(1)])
    return total + dot(right, weight[at(2)])


def own_row_body(core, hint, pair, weight, bias, features, mask, partial, odd_weight, features_out):
    pair_row = 2 - 2 * core[0]
    partial[...] = (
        taps(turned(hint), weight, 1)
        + taps(turned(pair), weight, pair_row)
        + bias[...].reshape(1, partial.shape[1])
    )
    odd_weight[...] = weight[2 - pair_row]
    features_out[...] = turned(features)


def merge_body(
    partial, odd, odd_weight, zero_weight, zero_bias, features, gather_low, gather_high, spread_low, merged_out, stats_out
):
    conv = partial[...] + taps(turned(odd), odd_weight, None)
    control = (conv / (1.0 + jnp.exp(-conv))).astype(BF16)
    branch = dot(control, zero_weight[...]) + zero_bias[...].reshape(1, partial.shape[1])
    merged = (features[...] + branch).astype(BF16)
    merged_out[...] = merged
    wide = merged.astype(F32)
    tokens, channels = wide.shape
    entries = tokens * (channels // GROUPS)
    mean = masked_sums(jnp.sum(wide, axis=0, keepdims=True), gather_low[...]) / entries
    centred = wide - masked_sums(mean, spread_low[...])
    square = masked_sums(jnp.sum(centred * centred, axis=0, keepdims=True), gather_high[...])
    stats_out[...] = jnp.broadcast_to(mean + square / entries, stats_out.shape)


def project_body(
    stats, merged, group_gain, proj_in, norm_gain, wq, wk, wv, spread_low, spread_high, inner_out, send
):
    channels = merged.shape[1]
    head_dim = channels // HEADS
    everyone = stats[...]
    average = jnp.mean(everyone, axis=0, keepdims=True)
    between = jnp.mean(jnp.square(everyone - average), axis=0, keepdims=True)
    mean = masked_sums(average, spread_low[...])
    variance = masked_sums(average, spread_high[...]) + masked_sums(between, spread_low[...])
    factor = lax.rsqrt(variance + NORM_EPS)
    grouped = ((merged[...].astype(F32) - mean) * factor * group_gain[...].reshape(1, channels)).astype(BF16)
    inner = dot(grouped, proj_in[...]).astype(BF16)
    inner_out[...] = inner
    wide = inner.astype(F32)
    centred = wide - jnp.mean(wide, axis=1, keepdims=True)
    variance = jnp.mean(centred * centred, axis=1, keepdims=True)
    normed = (centred * lax.rsqrt(variance + LAYER_EPS) * norm_gain[...].reshape(1, channels)).astype(BF16)
    scale = math.log2(math.e) / math.sqrt(head_dim)
    queries = (dot(normed, wq[...]) * scale).T
    keys = dot(normed, wk[...]).T
    values = dot(normed, wv[...]).T
    for h in range(HEADS):
        rows = slice(h * head_dim, (h + 1) * head_dim)
        block = jnp.concatenate([queries[rows], keys[rows], values[rows]], axis=0)
        send[h] = block.astype(BF16)


def squared(vectors):
    wide = vectors.astype(F32)
    return jnp.sum(wide * wide, axis=0, keepdims=True)


def attend_body(head_dim, first, n_queries, n_pieces, *refs):
    query_refs, refs = refs[:n_queries], refs[n_queries:]
    pieces, refs = refs[:n_pieces], refs[n_pieces:]
    if not first:
        states, refs = refs[:n_queries], refs[n_queries:]
    depth = head_dim + 8
    side_by_side = lambda ref: jnp.concatenate([ref[b] for b in range(ref.shape[0])], axis=1)
    pairs = [side_by_side(piece) for piece in pieces]
    keys = [pair[:depth].astype(F32).T.astype(BF16) for pair in pairs]
    ones = jnp.ones((16, pairs[0].shape[1]), BF16)
    summed = jnp.concatenate([jnp.concatenate([pair, ones], axis=0) for pair in pairs], axis=1)
    rows = summed.shape[0] - head_dim
    squares = functools.reduce(jnp.maximum, [squared(pair[:head_dim]) for pair in pairs])
    longest = jnp.sqrt(jnp.max(squares, axis=1, keepdims=True)) * (1.0 + 2.0**-10)
    for n, query_ref in enumerate(query_refs):
        queries = side_by_side(query_ref)
        bound = jnp.sqrt(squared(queries)) * longest
        queries = jnp.concatenate([queries, jnp.zeros((8, queries.shape[1]), BF16)], axis=0)

        def store(top, probs):
            if not first:
                before = states[n][rows : rows + 1, :]
                new_top = jnp.maximum(top, before)
            else:
                new_top = top
            total = dot(summed, jnp.concatenate(probs, axis=0))[head_dim:]
            if not first:
                total = total * jnp.exp2(top - new_top) + states[n][:rows, :] * jnp.exp2(before - new_top)
            refs[n][:rows, :] = total
            refs[n][rows:, :] = jnp.broadcast_to(new_top, (8, new_top.shape[1]))

        safe = jnp.max(bound) <= BOUND_LIMIT

        @pl.when(safe)
        def _():
            store(bound, [jnp.exp2(dot(k, queries) - bound).astype(BF16) for k in keys])

        @pl.when(jnp.logical_not(safe))
        def _():
            scores = [dot(k, queries) for k in keys]
            top = functools.reduce(jnp.maximum, [jnp.max(s, axis=0, keepdims=True) for s in scores])
            store(top, [jnp.exp2(s - top).astype(BF16) for s in scores])


def attend(queries, pieces, states, head_dim):
    blocks, _, tokens = queries[0].shape
    columns = blocks * tokens
    keys = sum(p.shape[0] * p.shape[2] for p in pieces) * len(queries)
    return call(
        functools.partial(attend_body, head_dim, states is None, len(queries), len(pieces)),
        [jax.ShapeDtypeStruct((head_dim + 24, columns), F32)] * len(queries),
        [*queries, *pieces, *(states or ())],
        limit=48,
        flops=2 * columns * keys * 512,
        read=keys * 160,
        trans=columns * keys,
    )


def combine_body(head_dim, mine, theirs, out):
    blocks, _, tokens = out.shape
    at = head_dim + 16
    a_top, b_top = mine[at : at + 1], theirs[at : at + 1]
    top = jnp.maximum(a_top, b_top)
    a_part, b_part = jnp.exp2(a_top - top), jnp.exp2(b_top - top)
    total = mine[head_dim : head_dim + 1] * a_part + theirs[head_dim : head_dim + 1] * b_part
    result = (mine[:head_dim] * a_part + theirs[:head_dim] * b_part) / total
    for b in range(blocks):
        out[b] = result[:, b * tokens : (b + 1) * tokens].astype(BF16)


def finish_body(attended, inner, merged, attn_out, proj_out, out):
    rows = turned(attended).astype(BF16)
    after = (inner[...].astype(F32) + dot(rows, attn_out[...])).astype(BF16)
    out[...] = (merged[...].astype(F32) + dot(after, proj_out[...])).T.astype(BF16)


def local(
    features,
    hint,
    conv_weight,
    conv_bias,
    zero_weight,
    zero_bias,
    group_gain,
    proj_in,
    norm_gain,
    query_weight,
    key_weight,
    value_weight,
    attn_out,
    proj_out,
):
    tokens, channels = features.shape
    head_dim = channels // HEADS
    everyone = lax.axis_size(SEQ)
    shape = jax.ShapeDtypeStruct
    hint, features = hint.T, features.T
    core = lax.axis_index("c").reshape(1)
    swap = [(0, 1), (1, 0)]
    ends = [(i, i + 1) for i in range(1, everyone - 1, 2)]
    odd = lax.ppermute(hint, SEQ, ends + [(b, a) for a, b in ends])
    pair = lax.ppermute(hint, "c", swap)
    masks = call(
        masks_body, [shape((channels, 128), BF16)] * 2 + [shape((128, channels), BF16)] * 2, (), flops=1000000000
    )
    partial, odd_weight, features = call(
        own_row_body,
        [shape((tokens, channels), F32), shape(conv_weight.shape[1:], BF16), shape((tokens, channels), F32)],
        (core, hint, pair, conv_weight, conv_bias, features, masks[0]),
        smem=1,
        flops=2 * tokens * channels * channels * 6,
        read=10 * channels * channels * 2,
    )
    merged, stats = call(
        merge_body,
        [shape((tokens, channels), BF16), shape((everyone, 128), F32)],
        (partial, odd, odd_weight, zero_weight, zero_bias, features, *masks[:3]),
        flops=2 * tokens * channels * channels * 4,
        read=4 * channels * channels * 2,
    )
    chain = range(lax.axis_size("z"))
    folded = [[*chain[::2], *chain[1::2][::-1]]]
    lines, cores = lax.axis_size("x"), lax.axis_size("c")
    whole = [[(x * len(chain) + z) * cores + c for x in range(lines) for z in folded[0] for c in range(cores)]]
    stats = lax.all_to_all(stats, SEQ, 0, 0, axis_index_groups=whole, tiled=True)
    inner, send = call(
        project_body,
        [shape((tokens, channels), BF16), shape((HEADS, 3 * head_dim, tokens), BF16)],
        (stats, merged, group_gain, proj_in, norm_gain, query_weight, key_weight, value_weight, *masks[2:]),
        flops=2 * tokens * channels * channels * 4,
        read=4 * channels * channels * 2,
    )
    received = lax.all_to_all(send, "z", 0, 0, axis_index_groups=folded, tiled=True)
    queries, pair = received[:, :head_dim, :], received[:, head_dim:, :]
    chips = lax.axis_size("x")
    ring = lambda by: [(i, (i + by) % chips) for i in range(chips)]
    pieces = [lax.ppermute(pair, "x", ring(by)) for by in (chips - 1, 2, 1)]
    others = lax.ppermute(queries, "c", swap)
    state = attend([queries], [pair], None, head_dim)
    other_state = attend([others], [pair, pieces[2]], None, head_dim)
    (theirs,) = attend([others], pieces[:2], other_state, head_dim)
    back = lax.ppermute(theirs, "c", swap)
    (mine,) = attend([queries], pieces, state, head_dim)
    result = call(
        functools.partial(combine_body, head_dim), shape((HEADS, head_dim, tokens), BF16), (mine, back)
    )
    attended = lax.all_to_all(result, "z", 0, 0, axis_index_groups=folded, tiled=True).reshape(channels, tokens)
    return call(
        finish_body,
        shape((channels, tokens), BF16),
        (attended, inner, merged, attn_out, proj_out),
        flops=2 * tokens * channels * channels * 2,
        read=2 * channels * channels * 2,
    ).T


def solution(mesh):
    torus = Mesh(mesh.devices.reshape(mesh.shape["dp"], 4, 8, 2), DP_SEQ)
    return jax.shard_map(
        local,
        mesh=torus,
        in_specs=(P(DP_SEQ, None), P(DP_SEQ, None)) + (P(),) * 12,
        out_specs=P(DP_SEQ, None),
        check_vma=False,
    )
```

```python
import functools
import math

import jax
import jax.numpy as jnp
from jax import lax
from jax.experimental import pallas as pl
from jax.experimental.pallas import tpu as pltpu
from jax.sharding import Mesh
from jax.sharding import PartitionSpec as P

HEADS = 8
GROUPS = 32
WIDTH = 128
SEQ = ("x", "z", "c")
DP_SEQ = ("dp", "x", "z", "c")
NORM_EPS = 1e-06
LAYER_EPS = 1e-05
BOUND_LIMIT = 56.0
F32 = jnp.float32
BF16 = jnp.bfloat16
VMEM = pl.BlockSpec(memory_space=pltpu.VMEM)
SMEM = pl.BlockSpec(memory_space=pltpu.SMEM)
MIB = 1024 * 1024


def dot(a, b):
    return jnp.dot(a, b, preferred_element_type=F32)


def masked_sums(row, mask):
    high = row.astype(BF16).astype(F32)
    middle = (row - high).astype(BF16).astype(F32)
    low = row - high - middle
    parts = jnp.concatenate([high, middle, low, jnp.zeros((5, row.shape[1]), F32)], axis=0).astype(BF16)
    return jnp.sum(dot(parts, mask), axis=0, keepdims=True)


def call(body, out_shape, args, scratch=(), limit=24, flops=0, read=0, trans=0, smem=0):
    many = isinstance(out_shape, (list, tuple))
    return pl.pallas_call(
        body,
        out_shape=out_shape,
        in_specs=[SMEM] * smem + [VMEM] * (len(args) - smem),
        out_specs=[VMEM] * len(out_shape) if many else VMEM,
        scratch_shapes=scratch,
        compiler_params=pltpu.CompilerParams(vmem_limit_bytes=limit * MIB),
        cost_estimate=pl.CostEstimate(flops=flops, bytes_accessed=read, transcendentals=trans),
    )(*args)


def group_spread(channels, lanes, first):
    per_group = channels // GROUPS
    lane = lax.broadcasted_iota(jnp.int32, (lanes, channels), 0)
    chan = lax.broadcasted_iota(jnp.int32, (lanes, channels), 1)
    low = (lane - first) * per_group
    inside = (chan >= low) & (chan < low + per_group) & (lane >= first) & (lane < first + GROUPS)
    return inside.astype(F32).astype(BF16)


def group_gather(channels, lanes, first):
    per_group = channels // GROUPS
    lane = lax.broadcasted_iota(jnp.int32, (channels, lanes), 1)
    chan = lax.broadcasted_iota(jnp.int32, (channels, lanes), 0)
    low = (lane - first) * per_group
    inside = (chan >= low) & (chan < low + per_group) & (lane >= first) & (lane < first + GROUPS)
    return inside.astype(F32).astype(BF16)


def turned(ref):
    return ref[...].astype(F32).T


def masks_body(gather_low, gather_high, spread_low, spread_high):
    channels, lanes = gather_low.shape
    gather_low[...] = group_gather(channels, lanes, 0)
    gather_high[...] = group_gather(channels, lanes, GROUPS)
    spread_low[...] = group_spread(channels, lanes, 0)
    spread_high[...] = group_spread(channels, lanes, GROUPS)


def taps(wide, weight, index):
    tokens, channels = wide.shape
    column = lax.broadcasted_iota(jnp.int32, (tokens, channels), 0)
    left = jnp.where(column == 0, 0.0, pltpu.roll(wide, 1, 0)).astype(BF16)
    right = jnp.where(column == tokens - 1, 0.0, pltpu.roll(wide, tokens - 1, 0)).astype(BF16)
    at = (lambda b: b) if index is None else (lambda b: (index, b))
    total = dot(left, weight[at(0)])
    total += dot(wide.astype(BF16), weight[at(1)])
    return total + dot(right, weight[at(2)])


def own_row_body(core, hint, pair, weight, bias, features, mask, partial, odd_weight, features_out):
    pair_row = 2 - 2 * core[0]
    partial[...] = (
        taps(turned(hint), weight, 1)
        + taps(turned(pair), weight, pair_row)
        + bias[...].reshape(1, partial.shape[1])
    )
    odd_weight[...] = weight[2 - pair_row]
    features_out[...] = turned(features)


def merge_body(
    partial, odd, odd_weight, zero_weight, zero_bias, features, gather_low, gather_high, spread_low, merged_out, stats_out
):
    conv = partial[...] + taps(turned(odd), odd_weight, None)
    control = (conv / (1.0 + jnp.exp(-conv))).astype(BF16)
    branch = dot(control, zero_weight[...]) + zero_bias[...].reshape(1, partial.shape[1])
    merged = (features[...] + branch).astype(BF16)
    merged_out[...] = merged
    wide = merged.astype(F32)
    tokens, channels = wide.shape
    entries = tokens * (channels // GROUPS)
    mean = masked_sums(jnp.sum(wide, axis=0, keepdims=True), gather_low[...]) / entries
    centred = wide - masked_sums(mean, spread_low[...])
    square = masked_sums(jnp.sum(centred * centred, axis=0, keepdims=True), gather_high[...])
    stats_out[...] = jnp.broadcast_to(mean + square / entries, stats_out.shape)


def project_body(
    stats, merged, group_gain, proj_in, norm_gain, wq, wk, wv, spread_low, spread_high, inner_out, send
):
    channels = merged.shape[1]
    head_dim = channels // HEADS
    everyone = stats[...]
    average = jnp.mean(everyone, axis=0, keepdims=True)
    between = jnp.mean(jnp.square(everyone - average), axis=0, keepdims=True)
    mean = masked_sums(average, spread_low[...])
    variance = masked_sums(average, spread_high[...]) + masked_sums(between, spread_low[...])
    factor = lax.rsqrt(variance + NORM_EPS)
    grouped = ((merged[...].astype(F32) - mean) * factor * group_gain[...].reshape(1, channels)).astype(BF16)
    inner = dot(grouped, proj_in[...]).astype(BF16)
    inner_out[...] = inner
    wide = inner.astype(F32)
    centred = wide - jnp.mean(wide, axis=1, keepdims=True)
    variance = jnp.mean(centred * centred, axis=1, keepdims=True)
    normed = (centred * lax.rsqrt(variance + LAYER_EPS) * norm_gain[...].reshape(1, channels)).astype(BF16)
    scale = math.log2(math.e) / math.sqrt(head_dim)
    queries = (dot(normed, wq[...]) * scale).T
    keys = dot(normed, wk[...]).T
    values = dot(normed, wv[...]).T
    for h in range(HEADS):
        rows = slice(h * head_dim, (h + 1) * head_dim)
        block = jnp.concatenate([queries[rows], keys[rows], values[rows]], axis=0)
        send[h] = block.astype(BF16)


def squared(vectors):
    wide = vectors.astype(F32)
    return jnp.sum(wide * wide, axis=0, keepdims=True)


def attend_body(head_dim, first, n_queries, n_pieces, *refs):
    query_refs, refs = refs[:n_queries], refs[n_queries:]
    pieces, refs = refs[:n_pieces], refs[n_pieces:]
    if not first:
        states, refs = refs[:n_queries], refs[n_queries:]
    depth = head_dim + 8
    side_by_side = lambda ref: jnp.concatenate([ref[b] for b in range(ref.shape[0])], axis=1)
    pairs = [side_by_side(piece) for piece in pieces]
    keys = [pair[:depth].astype(F32).T.astype(BF16) for pair in pairs]
    ones = jnp.ones((16, pairs[0].shape[1]), BF16)
    summed = jnp.concatenate([jnp.concatenate([pair, ones], axis=0) for pair in pairs], axis=1)
    rows = summed.shape[0] - head_dim
    squares = functools.reduce(jnp.maximum, [squared(pair[:head_dim]) for pair in pairs])
    longest = jnp.sqrt(jnp.max(squares, axis=1, keepdims=True)) * (1.0 + 2.0**-10)
    for n, query_ref in enumerate(query_refs):
        queries = side_by_side(query_ref)
        bound = jnp.sqrt(squared(queries)) * longest
        queries = jnp.concatenate([queries, jnp.zeros((8, queries.shape[1]), BF16)], axis=0)

        def store(top, probs):
            if not first:
                before = states[n][rows : rows + 1, :]
                new_top = jnp.maximum(top, before)
            else:
                new_top = top
            total = dot(summed, jnp.concatenate(probs, axis=0))[head_dim:]
            if not first:
                total = total * jnp.exp2(top - new_top) + states[n][:rows, :] * jnp.exp2(before - new_top)
            refs[n][:rows, :] = total
            refs[n][rows:, :] = jnp.broadcast_to(new_top, (8, new_top.shape[1]))

        safe = jnp.max(bound) <= BOUND_LIMIT

        @pl.when(safe)
        def _():
            store(bound, [jnp.exp2(dot(k, queries) - bound).astype(BF16) for k in keys])

        @pl.when(jnp.logical_not(safe))
        def _():
            scores = [dot(k, queries) for k in keys]
            top = functools.reduce(jnp.maximum, [jnp.max(s, axis=0, keepdims=True) for s in scores])
            store(top, [jnp.exp2(s - top).astype(BF16) for s in scores])


def attend(queries, pieces, states, head_dim):
    blocks, _, tokens = queries[0].shape
    columns = blocks * tokens
    keys = sum(p.shape[0] * p.shape[2] for p in pieces) * len(queries)
    return call(
        functools.partial(attend_body, head_dim, states is None, len(queries), len(pieces)),
        [jax.ShapeDtypeStruct((head_dim + 24, columns), F32)] * len(queries),
        [*queries, *pieces, *(states or ())],
        limit=48,
        flops=2 * columns * keys * 512,
        read=keys * 160,
        trans=columns * keys,
    )


def combine_body(head_dim, mine, theirs, out):
    blocks, _, tokens = out.shape
    at = head_dim + 16
    a_top, b_top = mine[at : at + 1], theirs[at : at + 1]
    top = jnp.maximum(a_top, b_top)
    a_part, b_part = jnp.exp2(a_top - top), jnp.exp2(b_top - top)
    total = mine[head_dim : head_dim + 1] * a_part + theirs[head_dim : head_dim + 1] * b_part
    result = (mine[:head_dim] * a_part + theirs[:head_dim] * b_part) / total
    for b in range(blocks):
        out[b] = result[:, b * tokens : (b + 1) * tokens].astype(BF16)


def finish_body(attended, inner, merged, attn_out, proj_out, out):
    rows = turned(attended).astype(BF16)
    after = (inner[...].astype(F32) + dot(rows, attn_out[...])).astype(BF16)
    out[...] = (merged[...].astype(F32) + dot(after, proj_out[...])).T.astype(BF16)


def local(
    features,
    hint,
    conv_weight,
    conv_bias,
    zero_weight,
    zero_bias,
    group_gain,
    proj_in,
    norm_gain,
    query_weight,
    key_weight,
    value_weight,
    attn_out,
    proj_out,
):
    tokens, channels = features.shape
    head_dim = channels // HEADS
    everyone = lax.axis_size(SEQ)
    shape = jax.ShapeDtypeStruct
    hint, features = hint.T, features.T
    core = lax.axis_index("c").reshape(1)
    swap = [(0, 1), (1, 0)]
    ends = [(i, i + 1) for i in range(1, everyone - 1, 2)]
    odd = lax.ppermute(hint, SEQ, ends + [(b, a) for a, b in ends])
    pair = lax.ppermute(hint, "c", swap)
    masks = call(
        masks_body, [shape((channels, 128), BF16)] * 2 + [shape((128, channels), BF16)] * 2, (), flops=1000000000
    )
    partial, odd_weight, features = call(
        own_row_body,
        [shape((tokens, channels), F32), shape(conv_weight.shape[1:], BF16), shape((tokens, channels), F32)],
        (core, hint, pair, conv_weight, conv_bias, features, masks[0]),
        smem=1,
        flops=2 * tokens * channels * channels * 6,
        read=10 * channels * channels * 2,
    )
    merged, stats = call(
        merge_body,
        [shape((tokens, channels), BF16), shape((everyone, 128), F32)],
        (partial, odd, odd_weight, zero_weight, zero_bias, features, *masks[:3]),
        flops=2 * tokens * channels * channels * 4,
        read=4 * channels * channels * 2,
    )
    chain = range(lax.axis_size("z"))
    folded = [[*chain[::2], *chain[1::2][::-1]]]
    lines, cores = lax.axis_size("x"), lax.axis_size("c")
    whole = [[(x * len(chain) + z) * cores + c for x in range(lines) for z in folded[0] for c in range(cores)]]
    stats = lax.all_to_all(stats, SEQ, 0, 0, axis_index_groups=whole, tiled=True)
    inner, send = call(
        project_body,
        [shape((tokens, channels), BF16), shape((HEADS, 3 * head_dim, tokens), BF16)],
        (stats, merged, group_gain, proj_in, norm_gain, query_weight, key_weight, value_weight, *masks[2:]),
        flops=2 * tokens * channels * channels * 4,
        read=4 * channels * channels * 2,
    )
    received = lax.all_to_all(send, "z", 0, 0, axis_index_groups=folded, tiled=True)
    queries, pair = received[:, :head_dim, :], received[:, head_dim:, :]
    chips = lax.axis_size("x")
    ring = lambda by: [(i, (i + by) % chips) for i in range(chips)]
    pieces = [lax.ppermute(pair, "x", ring(by)) for by in (2, chips - 1, 1)]
    others = lax.ppermute(queries, "c", swap)
    state = attend([queries], [pair], None, head_dim)
    other_state = attend([others], [pair, pieces[2]], None, head_dim)
    (theirs,) = attend([others], pieces[:2], other_state, head_dim)
    back = lax.ppermute(theirs, "c", swap)
    (mine,) = attend([queries], pieces, state, head_dim)
    result = call(
        functools.partial(combine_body, head_dim), shape((HEADS, head_dim, tokens), BF16), (mine, back)
    )
    attended = lax.all_to_all(result, "z", 0, 0, axis_index_groups=folded, tiled=True).reshape(channels, tokens)
    return call(
        finish_body,
        shape((channels, tokens), BF16),
        (attended, inner, merged, attn_out, proj_out),
        flops=2 * tokens * channels * channels * 2,
        read=2 * channels * channels * 2,
    ).T


def solution(mesh):
    torus = Mesh(mesh.devices.reshape(mesh.shape["dp"], 4, 8, 2), DP_SEQ)
    return jax.shard_map(
        local,
        mesh=torus,
        in_specs=(P(DP_SEQ, None), P(DP_SEQ, None)) + (P(),) * 12,
        out_specs=P(DP_SEQ, None),
        check_vma=False,
    )
```

```python
import functools
import math

import jax
import jax.numpy as jnp
from jax import lax
from jax.experimental import pallas as pl
from jax.experimental.pallas import tpu as pltpu
from jax.sharding import Mesh
from jax.sharding import PartitionSpec as P

HEADS = 8
GROUPS = 32
WIDTH = 128
SEQ = ("x", "z", "c")
DP_SEQ = ("dp", "x", "z", "c")
NORM_EPS = 1e-06
LAYER_EPS = 1e-05
BOUND_LIMIT = 56.0
F32 = jnp.float32
BF16 = jnp.bfloat16
VMEM = pl.BlockSpec(memory_space=pltpu.VMEM)
SMEM = pl.BlockSpec(memory_space=pltpu.SMEM)
MIB = 1024 * 1024


def dot(a, b):
    return jnp.dot(a, b, preferred_element_type=F32)


def masked_sums(row, mask):
    high = row.astype(BF16).astype(F32)
    middle = (row - high).astype(BF16).astype(F32)
    low = row - high - middle
    parts = jnp.concatenate([high, middle, low, jnp.zeros((5, row.shape[1]), F32)], axis=0).astype(BF16)
    return jnp.sum(dot(parts, mask), axis=0, keepdims=True)


def call(body, out_shape, args, scratch=(), limit=24, flops=0, read=0, trans=0, smem=0):
    many = isinstance(out_shape, (list, tuple))
    return pl.pallas_call(
        body,
        out_shape=out_shape,
        in_specs=[SMEM] * smem + [VMEM] * (len(args) - smem),
        out_specs=[VMEM] * len(out_shape) if many else VMEM,
        scratch_shapes=scratch,
        compiler_params=pltpu.CompilerParams(vmem_limit_bytes=limit * MIB),
        cost_estimate=pl.CostEstimate(flops=flops, bytes_accessed=read, transcendentals=trans),
    )(*args)


def group_spread(channels, lanes, first):
    per_group = channels // GROUPS
    lane = lax.broadcasted_iota(jnp.int32, (lanes, channels), 0)
    chan = lax.broadcasted_iota(jnp.int32, (lanes, channels), 1)
    low = (lane - first) * per_group
    inside = (chan >= low) & (chan < low + per_group) & (lane >= first) & (lane < first + GROUPS)
    return inside.astype(F32).astype(BF16)


def group_gather(channels, lanes, first):
    per_group = channels // GROUPS
    lane = lax.broadcasted_iota(jnp.int32, (channels, lanes), 1)
    chan = lax.broadcasted_iota(jnp.int32, (channels, lanes), 0)
    low = (lane - first) * per_group
    inside = (chan >= low) & (chan < low + per_group) & (lane >= first) & (lane < first + GROUPS)
    return inside.astype(F32).astype(BF16)


def turned(ref):
    return ref[...].astype(F32).T


def masks_body(gather_low, gather_high, spread_low, spread_high):
    channels, lanes = gather_low.shape
    gather_low[...] = group_gather(channels, lanes, 0)
    gather_high[...] = group_gather(channels, lanes, GROUPS)
    spread_low[...] = group_spread(channels, lanes, 0)
    spread_high[...] = group_spread(channels, lanes, GROUPS)


def taps(wide, weight, index):
    tokens, channels = wide.shape
    column = lax.broadcasted_iota(jnp.int32, (tokens, channels), 0)
    left = jnp.where(column == 0, 0.0, pltpu.roll(wide, 1, 0)).astype(BF16)
    right = jnp.where(column == tokens - 1, 0.0, pltpu.roll(wide, tokens - 1, 0)).astype(BF16)
    at = (lambda b: b) if index is None else (lambda b: (index, b))
    total = dot(left, weight[at(0)])
    total += dot(wide.astype(BF16), weight[at(1)])
    return total + dot(right, weight[at(2)])


def own_row_body(core, hint, pair, weight, bias, features, mask, partial, odd_weight, features_out):
    pair_row = 2 - 2 * core[0]
    partial[...] = (
        taps(turned(hint), weight, 1)
        + taps(turned(pair), weight, pair_row)
        + bias[...].reshape(1, partial.shape[1])
    )
    odd_weight[...] = weight[2 - pair_row]
    features_out[...] = turned(features)


def merge_body(
    partial, odd, odd_weight, zero_weight, zero_bias, features, gather_low, gather_high, spread_low, merged_out, stats_out
):
    conv = partial[...] + taps(turned(odd), odd_weight, None)
    control = (conv / (1.0 + jnp.exp(-conv))).astype(BF16)
    branch = dot(control, zero_weight[...]) + zero_bias[...].reshape(1, partial.shape[1])
    merged = (features[...] + branch).astype(BF16)
    merged_out[...] = merged
    wide = merged.astype(F32)
    tokens, channels = wide.shape
    entries = tokens * (channels // GROUPS)
    mean = masked_sums(jnp.sum(wide, axis=0, keepdims=True), gather_low[...]) / entries
    centred = wide - masked_sums(mean, spread_low[...])
    square = masked_sums(jnp.sum(centred * centred, axis=0, keepdims=True), gather_high[...])
    stats_out[...] = jnp.broadcast_to(mean + square / entries, stats_out.shape)


def project_body(
    stats, merged, group_gain, proj_in, norm_gain, wq, wk, wv, spread_low, spread_high, inner_out, send
):
    channels = merged.shape[1]
    head_dim = channels // HEADS
    everyone = stats[...]
    average = jnp.mean(everyone, axis=0, keepdims=True)
    between = jnp.mean(jnp.square(everyone - average), axis=0, keepdims=True)
    mean = masked_sums(average, spread_low[...])
    variance = masked_sums(average, spread_high[...]) + masked_sums(between, spread_low[...])
    factor = lax.rsqrt(variance + NORM_EPS)
    grouped = ((merged[...].astype(F32) - mean) * factor * group_gain[...].reshape(1, channels)).astype(BF16)
    inner = dot(grouped, proj_in[...]).astype(BF16)
    inner_out[...] = inner
    wide = inner.astype(F32)
    centred = wide - jnp.mean(wide, axis=1, keepdims=True)
    variance = jnp.mean(centred * centred, axis=1, keepdims=True)
    normed = (centred * lax.rsqrt(variance + LAYER_EPS) * norm_gain[...].reshape(1, channels)).astype(BF16)
    scale = math.log2(math.e) / math.sqrt(head_dim)
    queries = (dot(normed, wq[...]) * scale).T
    keys = dot(normed, wk[...]).T
    values = dot(normed, wv[...]).T
    for h in range(HEADS):
        rows = slice(h * head_dim, (h + 1) * head_dim)
        block = jnp.concatenate([queries[rows], keys[rows], values[rows]], axis=0)
        send[h] = block.astype(BF16)


def squared(vectors):
    wide = vectors.astype(F32)
    return jnp.sum(wide * wide, axis=0, keepdims=True)


def attend_body(head_dim, first, n_queries, n_pieces, *refs):
    query_refs, refs = refs[:n_queries], refs[n_queries:]
    pieces, refs = refs[:n_pieces], refs[n_pieces:]
    if not first:
        states, refs = refs[:n_queries], refs[n_queries:]
    depth = head_dim + 8
    side_by_side = lambda ref: jnp.concatenate([ref[b] for b in range(ref.shape[0])], axis=1)
    pairs = [side_by_side(piece) for piece in pieces]
    keys = [pair[:depth].astype(F32).T.astype(BF16) for pair in pairs]
    ones = jnp.ones((16, pairs[0].shape[1]), BF16)
    summed = jnp.concatenate([jnp.concatenate([pair, ones], axis=0) for pair in pairs], axis=1)
    rows = summed.shape[0] - head_dim
    squares = functools.reduce(jnp.maximum, [squared(pair[:head_dim]) for pair in pairs])
    longest = jnp.sqrt(jnp.max(squares, axis=1, keepdims=True)) * (1.0 + 2.0**-10)
    for n, query_ref in enumerate(query_refs):
        queries = side_by_side(query_ref)
        bound = jnp.sqrt(squared(queries)) * longest
        queries = jnp.concatenate([queries, jnp.zeros((8, queries.shape[1]), BF16)], axis=0)

        def store(top, probs):
            if not first:
                before = states[n][rows : rows + 1, :]
                new_top = jnp.maximum(top, before)
            else:
                new_top = top
            total = dot(summed, jnp.concatenate(probs, axis=0))[head_dim:]
            if not first:
                total = total * jnp.exp2(top - new_top) + states[n][:rows, :] * jnp.exp2(before - new_top)
            refs[n][:rows, :] = total
            refs[n][rows:, :] = jnp.broadcast_to(new_top, (8, new_top.shape[1]))

        safe = jnp.max(bound) <= BOUND_LIMIT

        @pl.when(safe)
        def _():
            store(bound, [jnp.exp2(dot(k, queries) - bound).astype(BF16) for k in keys])

        @pl.when(jnp.logical_not(safe))
        def _():
            scores = [dot(k, queries) for k in keys]
            top = functools.reduce(jnp.maximum, [jnp.max(s, axis=0, keepdims=True) for s in scores])
            store(top, [jnp.exp2(s - top).astype(BF16) for s in scores])


def attend(queries, pieces, states, head_dim):
    blocks, _, tokens = queries[0].shape
    columns = blocks * tokens
    keys = sum(p.shape[0] * p.shape[2] for p in pieces) * len(queries)
    return call(
        functools.partial(attend_body, head_dim, states is None, len(queries), len(pieces)),
        [jax.ShapeDtypeStruct((head_dim + 24, columns), F32)] * len(queries),
        [*queries, *pieces, *(states or ())],
        limit=48,
        flops=2 * columns * keys * 512,
        read=keys * 160,
        trans=columns * keys,
    )


def combine_body(head_dim, mine, theirs, out):
    blocks, _, tokens = out.shape
    at = head_dim + 16
    a_top, b_top = mine[at : at + 1], theirs[at : at + 1]
    top = jnp.maximum(a_top, b_top)
    a_part, b_part = jnp.exp2(a_top - top), jnp.exp2(b_top - top)
    total = mine[head_dim : head_dim + 1] * a_part + theirs[head_dim : head_dim + 1] * b_part
    result = (mine[:head_dim] * a_part + theirs[:head_dim] * b_part) / total
    for b in range(blocks):
        out[b] = result[:, b * tokens : (b + 1) * tokens].astype(BF16)


def finish_body(attended, inner, merged, attn_out, proj_out, out):
    rows = turned(attended).astype(BF16)
    after = (inner[...].astype(F32) + dot(rows, attn_out[...])).astype(BF16)
    out[...] = (merged[...].astype(F32) + dot(after, proj_out[...])).T.astype(BF16)


def local(
    features,
    hint,
    conv_weight,
    conv_bias,
    zero_weight,
    zero_bias,
    group_gain,
    proj_in,
    norm_gain,
    query_weight,
    key_weight,
    value_weight,
    attn_out,
    proj_out,
):
    tokens, channels = features.shape
    head_dim = channels // HEADS
    everyone = lax.axis_size(SEQ)
    shape = jax.ShapeDtypeStruct
    hint, features = hint.T, features.T
    core = lax.axis_index("c").reshape(1)
    swap = [(0, 1), (1, 0)]
    ends = [(i, i + 1) for i in range(1, everyone - 1, 2)]
    odd = lax.ppermute(hint, SEQ, ends + [(b, a) for a, b in ends])
    pair = lax.ppermute(hint, "c", swap)
    masks = call(
        masks_body, [shape((channels, 128), BF16)] * 2 + [shape((128, channels), BF16)] * 2, (), flops=1000000000
    )
    partial, odd_weight, features = call(
        own_row_body,
        [shape((tokens, channels), F32), shape(conv_weight.shape[1:], BF16), shape((tokens, channels), F32)],
        (core, hint, pair, conv_weight, conv_bias, features, masks[0]),
        smem=1,
        flops=2 * tokens * channels * channels * 6,
        read=10 * channels * channels * 2,
    )
    merged, stats = call(
        merge_body,
        [shape((tokens, channels), BF16), shape((everyone, 128), F32)],
        (partial, odd, odd_weight, zero_weight, zero_bias, features, *masks[:3]),
        flops=2 * tokens * channels * channels * 4,
        read=4 * channels * channels * 2,
    )
    chain = range(lax.axis_size("z"))
    folded = [[*chain[::2], *chain[1::2][::-1]]]
    lines, cores = lax.axis_size("x"), lax.axis_size("c")
    whole = [[(x * len(chain) + z) * cores + c for x in range(lines) for z in folded[0] for c in range(cores)]]
    stats = lax.all_to_all(stats, SEQ, 0, 0, axis_index_groups=whole, tiled=True)
    inner, send = call(
        project_body,
        [shape((tokens, channels), BF16), shape((HEADS, 3 * head_dim, tokens), BF16)],
        (stats, merged, group_gain, proj_in, norm_gain, query_weight, key_weight, value_weight, *masks[2:]),
        flops=2 * tokens * channels * channels * 4,
        read=4 * channels * channels * 2,
    )
    received = lax.all_to_all(send, "z", 0, 0, axis_index_groups=folded, tiled=True)
    queries, pair = received[:, :head_dim, :], received[:, head_dim:, :]
    chips = lax.axis_size("x")
    ring = lambda by: [(i, (i + by) % chips) for i in range(chips)]
    pieces = [lax.ppermute(pair, "x", ring(by)) for by in (2, chips - 1, 1)]
    others = lax.ppermute(queries, "c", swap)
    state = attend([queries], [pair], None, head_dim)
    other_state = attend([others], [pair, pieces[2]], None, head_dim)
    other_state = attend([others], pieces[1:2], other_state, head_dim)
    (theirs,) = attend([others], pieces[:1], other_state, head_dim)
    back = lax.ppermute(theirs, "c", swap)
    (mine,) = attend([queries], pieces, state, head_dim)
    result = call(
        functools.partial(combine_body, head_dim), shape((HEADS, head_dim, tokens), BF16), (mine, back)
    )
    attended = lax.all_to_all(result, "z", 0, 0, axis_index_groups=folded, tiled=True).reshape(channels, tokens)
    return call(
        finish_body,
        shape((channels, tokens), BF16),
        (attended, inner, merged, attn_out, proj_out),
        flops=2 * tokens * channels * channels * 2,
        read=2 * channels * channels * 2,
    ).T


def solution(mesh):
    torus = Mesh(mesh.devices.reshape(mesh.shape["dp"], 4, 8, 2), DP_SEQ)
    return jax.shard_map(
        local,
        mesh=torus,
        in_specs=(P(DP_SEQ, None), P(DP_SEQ, None)) + (P(),) * 12,
        out_specs=P(DP_SEQ, None),
        check_vma=False,
    )
```
